32 devices in a mesh: dp: 4 (over z), ctx: 4 (over y, x), tensor: 2 (over core).
Axes of the slice: x: 2, y: 2, z: 4, core: 2. Of those that a mesh axis runs over, the one named last changes fastest.
Arguments:
- query_rows: bfloat16 [4, 512, 4096], P('dp', 'ctx', 'tensor'), may hold values from -200 to 200
- key_rows: bfloat16 [4, 512, 256], P('dp', 'ctx'), may hold values from -6 to 6
- value_rows: bfloat16 [4, 512, 256], P('dp', 'ctx'), may hold values from -6 to 6
- residual: bfloat16 [4, 512, 4096], P('dp', ('ctx', 'tensor')), may hold values from -6 to 6
- out_proj: bfloat16 [4096, 4096], P('tensor'), may hold values from -0.09375 to 0.09375
- post_gain: bfloat16 [4096], replicated, may hold values from 0.099609375 to 1.8984375
- router: bfloat16 [4096, 16], replicated, may hold values from -10 to 10
- routes: int32 [4, 512, 8], P('dp', ('ctx', 'tensor')), may hold values from 0 to 15, all different within a row; in each aligned block of 64 rows (0 to 63, 64 to 127, ..., all dimensions but the last counted through in order) at most 64 rows name the same one
- w_gate: bfloat16 [16, 4096, 1536], P(('ctx', 'tensor'), None, 'dp'), may hold values from -0.09375 to 0.09375
- w_up: bfloat16 [16, 4096, 1536], P(('ctx', 'tensor'), None, 'dp'), may hold values from -0.09375 to 0.09375
- w_down: bfloat16 [16, 1536, 4096], P(('ctx', 'tensor'), 'dp'), may hold values from -80 to 80
Outputs:
- layer_out: bfloat16 [4, 512, 4096], P('dp', ('ctx', 'tensor'))
The draws below stay inside these ranges and needn't reach their ends.
Inputs may be any that keep to these rules, and one draw needn't show every extreme that they name: `routes`: the 8 experts of a token differ. Among the 64 tokens of one device (aligned blocks of the token rows), no expert is named by more than 64 of them, a bound that some block reaches.
All inputs are finite; a program needn't handle non-finite values.
Results may differ from the reference program's by a relative error of at most 0.014.
Values may be sent and summed in bfloat16 or wider, within the bound.
No kernel may reach another device: no remote copies, remote signals or barrier semaphores. Data moves between devices by JAX's collectives and lax.ppermute only.
A program may use at most 192 MiB of HBM per device.

```python
import math
import jax
import jax.numpy as jnp
import numpy as np
from jax import lax

D = 4096
QH = 32
KVH = 2
HEAD_WIDTH = 128
FF = 1536
TOP = 8
SEQ = 512
TOK_DEV = 64
EXPERTS = 16
FF_DEV = 384
CAP = 64
N_DP = 4
N_CTX = 4
N_TENSOR = 2


def shared_keys(key):
    return jnp.clip(jax.random.normal(key, (N_DP, SEQ, KVH * HEAD_WIDTH), jnp.float32), -6.0, 6.0)


def expert_kinds(key):
    ranking = jax.random.permutation(jax.random.fold_in(key, 101), EXPERTS)
    return ranking < max(1, EXPERTS // 4)


def channel_kinds(key):
    ranking = jax.random.permutation(jax.random.fold_in(key, 103), D)
    fixed_count = max(1, D // 512)
    fixed_set = ranking < fixed_count
    return fixed_set


def channel_pushes():
    fixed_count = max(1, D // 512)
    fixed_rms = math.sqrt(0.25 * (D - fixed_count) / D + fixed_count * 16.0 / D)
    push_down = 4.0 * fixed_rms / (fixed_count * 4.0)
    return push_down


def draw_key_rows(key, part):
    base = shared_keys(key)
    return base.astype(jnp.bfloat16)


def draw_query_rows(key, part):
    key = jax.random.fold_in(key, 7)
    drawn = jnp.clip(jax.random.normal(key, (N_DP, SEQ, QH * HEAD_WIDTH), jnp.float32), -6.0, 6.0)
    return drawn.astype(jnp.bfloat16)


def draw_residual(key, part):
    fixed_set = channel_kinds(key)
    key = jax.random.fold_in(key, 11)
    jitter = 0.5 * jnp.clip(jax.random.normal(key, (N_DP, SEQ, D), jnp.float32), -6.0, 6.0)
    stream_vals = jitter
    stream_vals = jnp.where(fixed_set[None, None, :], 4.0 + 0.5 * jitter, stream_vals)
    return stream_vals.astype(jnp.bfloat16)


def draw_router(key, part):
    loud_set = expert_kinds(key)
    fixed_set = channel_kinds(key)
    push_down = channel_pushes()
    key = jax.random.fold_in(key, 5)
    column_scale = jnp.where(loud_set, 0.2, 0.7)
    jitter = jnp.clip(jax.random.normal(key, (D, EXPERTS), jnp.float32), -6.0, 6.0)
    jitter = jitter * column_scale[None, :] / math.sqrt(D)
    offsets = jnp.where(jnp.logical_and(fixed_set[:, None], loud_set[None, :]), -push_down, 0.0)
    return (jitter + offsets).astype(jnp.bfloat16)


def draw_w_down(key, part):
    loud_set = expert_kinds(key)
    key = jax.random.fold_in(key, 13)
    entries = jnp.clip(jax.random.normal(key, (EXPERTS, FF, D), jnp.float32), -6.0, 6.0) / math.sqrt(FF)
    factor = jnp.where(loud_set, 100.0, 1.0)
    return (entries * factor[:, None, None]).astype(jnp.bfloat16)


def block_levels(key, shape, split, low, top_value):
    level = 1.0
    for dim, shards_of in split:
        draws = jax.random.uniform(jax.random.fold_in(jax.random.fold_in(key, 6), dim), (shards_of,), jnp.float32, low / len(split), top_value / len(split))
        level = level * jnp.repeat(jnp.exp(draws), shape[dim] // shards_of).reshape((-1,) + (1,) * (len(shape) - 1 - dim))
    return level


def shared_out(key, own, number, rows, number_of, top, bound, slope):
    sequence = jax.random.permutation(key, number_of)
    heavy_load, ordinary = portions_of(number_of, rows * top, bound, slope, True), portions_of(number_of, rows * top, bound, slope, False)
    places = jnp.arange(number_of)

    def named(lengths, rotation):
        used = int((lengths > 0).sum())
        fixed = max(1, used // 4)
        moved = fixed + (places - fixed + rotation * (used - fixed)) % max(1, number_of - fixed)
        return jnp.zeros((number_of,), jnp.int32).at[sequence[jnp.where(places < fixed, places, moved)]].set(jnp.asarray(lengths, jnp.int32))

    lengths = jnp.where(number % 4 == 0, named(heavy_load, number // 4), named(ordinary, number - number // 4 - 1))
    mixed = jax.random.permutation(jax.random.fold_in(own, 3), number_of)
    giver, receiver = mixed[0:number_of // 2 * 2:2], mixed[1:number_of // 2 * 2:2]
    room = jnp.minimum(lengths[giver] - 1, bound - lengths[receiver]) // 2
    room = jnp.where((giver == sequence[0]) | (receiver == sequence[0]) | (lengths[receiver] == 0), 0, jnp.maximum(room, 0))
    moved = jax.random.randint(jax.random.fold_in(own, 4), (number_of // 2,), 0, 1 << 20) % (room + 1)
    lengths = lengths.at[giver].add(-moved).at[receiver].add(moved)
    labels = jnp.searchsorted(jnp.cumsum(lengths), jnp.arange(rows * top), side="right").astype(jnp.int32)
    table = labels.reshape(top, rows).T
    table = table[jax.random.permutation(jax.random.fold_in(own, 1), rows)]
    rotation = jax.random.randint(jax.random.fold_in(own, 2), (rows, 1), 0, top)
    return jnp.take_along_axis(table, (jnp.arange(top)[None, :] + rotation) % top, axis=1)


def portions_of(number_of, total, most, lean, full):
    weights = [(1 << 20) // math.isqrt(grade ** lean) + 1 for grade in range(1, number_of + 1)]
    largest = most if full else min(most, max(-(-total // number_of), total * weights[0] // sum(weights)))
    least = 1 if total - largest >= number_of - 1 else 0
    counts, surplus = [largest] + [least] * (number_of - 1), total - largest - least * (number_of - 1)
    while surplus > 0:
        candidates = [i for i in range(1, number_of) if counts[i] < largest] or [i for i in range(1, number_of) if counts[i] < most]
        whole, left = sum([weights[i] for i in candidates]), surplus
        for i in candidates:
            extra = min(most - counts[i], max(1, left * weights[i] // whole), surplus)
            counts[i] = counts[i] + extra
            surplus = surplus - extra
    return np.array(counts)


def normal_values(own_key, shape, deviation, reach, pieces=(), kind=jnp.bfloat16):
    values = jax.random.normal(own_key, shape, jnp.float32) * deviation
    if len(pieces) > 0:
        values = block_levels(own_key, shape, pieces, -0.22, 0.18) * values
    return jnp.clip(values, min=-reach, max=reach).astype(kind)


def setup_inputs(seed: int = 0) -> dict:
    arg_keys = jax.random.split(jax.random.key(seed), 12)
    query_rows = draw_query_rows(jax.random.fold_in(arg_keys[11], 71), 0)
    key_rows = draw_key_rows(jax.random.fold_in(arg_keys[11], 71), 0)
    value_rows = normal_values(arg_keys[2], (N_DP, SEQ, KVH * HEAD_WIDTH), 1.0, 6.0, ((0, 4), (1, 4)))
    residual = draw_residual(jax.random.fold_in(arg_keys[11], 71), 0)
    out_proj = normal_values(arg_keys[4], (QH * HEAD_WIDTH, D), (QH * HEAD_WIDTH) ** -0.5, 0.09375, ((0, 2),))
    post_gain = jnp.clip(1.0 + 0.18 * jax.random.normal(arg_keys[5], (D,), jnp.float32), 0.099609375, 1.8984375).astype(jnp.bfloat16)
    router = draw_router(jax.random.fold_in(arg_keys[11], 71), 0)
    routes_keys = jax.random.split(jax.random.fold_in(arg_keys[7], 1), N_DP * SEQ // TOK_DEV)
    routes_turns = jax.random.permutation(jax.random.fold_in(arg_keys[7], 3), N_DP * SEQ // TOK_DEV)
    routes = jax.vmap(lambda own, number: shared_out(jax.random.fold_in(arg_keys[7], 2), own, number, TOK_DEV, EXPERTS, TOP, CAP, 2))(routes_keys, routes_turns).reshape((N_DP, SEQ, TOP))
    w_gate = normal_values(arg_keys[8], (EXPERTS, D, FF), D ** -0.5, 0.09375, ((0, 8), (2, 4)))
    w_up = normal_values(arg_keys[9], (EXPERTS, D, FF), D ** -0.5, 0.09375, ((0, 8), (2, 4)))
    w_down = draw_w_down(jax.random.fold_in(arg_keys[11], 71), 0)
    return {"query_rows": query_rows, "key_rows": key_rows, "value_rows": value_rows, "residual": residual, "out_proj": out_proj, "post_gain": post_gain, "router": router, "routes": routes, "w_gate": w_gate, "w_up": w_up, "w_down": w_down}


def rotate(rows, heads, offset):
    batch, length, width = rows.shape
    values = rows.astype(jnp.float32).reshape(batch, length, heads, HEAD_WIDTH)
    half = HEAD_WIDTH // 2
    places = (offset + jnp.arange(length)).astype(jnp.float32)
    freqs = jnp.power(jnp.float32(1000000.0), -(jnp.arange(half).astype(jnp.float32) * 2.0 / HEAD_WIDTH))
    angles = places[:, None] * freqs[None, :]
    cosine = jnp.cos(angles)[None, :, None, :]
    sine = jnp.sin(angles)[None, :, None, :]
    first = values[..., :half]
    second = values[..., half:]
    turned = jnp.concatenate([first * cosine - second * sine, second * cosine + first * sine], axis=-1)
    return turned.astype(jnp.bfloat16)

def reference(query_rows, key_rows, value_rows, residual, out_proj, post_gain, router, routes, w_gate, w_up, w_down):
    group = QH // KVH
    qrot = rotate(query_rows, QH, 0)
    krot = rotate(key_rows, KVH, 0)
    values = value_rows.reshape(N_DP, SEQ, KVH, HEAD_WIDTH)
    causal = jnp.arange(SEQ)[:, None] >= jnp.arange(SEQ)[None, :]

    def one_head(head_id):
        head_query_rows = lax.dynamic_index_in_dim(qrot, head_id, 2, keepdims=False).astype(jnp.float32)
        head_key_rows = lax.dynamic_index_in_dim(krot, head_id // group, 2, keepdims=False).astype(jnp.float32)
        head_value_rows = lax.dynamic_index_in_dim(values, head_id // group, 2, keepdims=False).astype(jnp.float32)
        attention_score = jnp.einsum('pwv,phv->pwh', head_query_rows, head_key_rows) / jnp.sqrt(jnp.float32(HEAD_WIDTH))
        attention_score = jnp.where(causal[None], attention_score, jnp.float32(-1e+30))
        peak = lax.optimization_barrier(jnp.max(attention_score, axis=-1, keepdims=True))
        expon = jnp.where(causal[None], jnp.exp(attention_score - peak), jnp.float32(0.0))
        total = lax.optimization_barrier(jnp.sum(expon, axis=-1))
        softmax_weights = lax.optimization_barrier(expon.astype(jnp.bfloat16)).astype(jnp.float32)
        summed_output = jnp.einsum('gvj,gjw->gvw', softmax_weights, head_value_rows)
        return (summed_output / total[..., None]).astype(jnp.bfloat16)
    heads_out = lax.map(one_head, jnp.arange(QH))
    attended = jnp.transpose(heads_out, (1, 2, 0, 3)).reshape(N_DP * SEQ, QH * HEAD_WIDTH)
    projected = jnp.dot(attended, out_proj, preferred_element_type=jnp.float32)
    mixed = (residual.reshape(N_DP * SEQ, D).astype(jnp.float32) + projected).astype(jnp.bfloat16)
    mixed_wide = lax.optimization_barrier(mixed).astype(jnp.float32)
    scale = lax.rsqrt(lax.optimization_barrier(jnp.mean(mixed_wide * mixed_wide, axis=-1, keepdims=True)) + 1e-06)
    normed = (mixed_wide * scale * post_gain.astype(jnp.float32)).astype(jnp.bfloat16)
    logits = jnp.dot(normed, router, preferred_element_type=jnp.float32)
    flat_routes = routes.reshape(N_DP * SEQ, TOP)
    chosen = jnp.take_along_axis(logits, flat_routes, axis=1)
    gates = jax.nn.softmax(chosen, axis=-1)
    count_tokens = N_DP * SEQ
    limit = N_DP * N_CTX * N_TENSOR * CAP
    route_list = flat_routes.reshape(-1)
    gate_list = gates.reshape(-1)
    token_list = (jnp.arange(count_tokens * TOP) // TOP).astype(jnp.int32)
    padded = jnp.concatenate([normed, jnp.zeros((1, D), jnp.bfloat16)], axis=0)

    def one_expert(carry, inputs):
        gate_mat, up_mat, down_mat, expert_id = inputs
        struck = (route_list == expert_id).astype(jnp.int32)
        place = jnp.cumsum(struck) - 1
        place = jnp.where(struck > 0, place, limit).astype(jnp.int32)
        table = jnp.full((limit,), count_tokens, jnp.int32).at[place].set(token_list, mode='drop')
        weight_tab = jnp.zeros((limit,), jnp.float32).at[place].set(gate_list, mode='drop')
        rows = padded[table]
        gate_val = jnp.dot(rows, gate_mat, preferred_element_type=jnp.float32)
        up_val = jnp.dot(rows, up_mat, preferred_element_type=jnp.float32)
        hidden = (jax.nn.silu(gate_val) * up_val).astype(jnp.bfloat16)
        summed_output = jnp.zeros((limit, D), jnp.float32)
        for block in range(N_DP):
            part = jnp.dot(hidden[:, block * FF_DEV:(block + 1) * FF_DEV], down_mat[block * FF_DEV:(block + 1) * FF_DEV], preferred_element_type=jnp.float32).astype(jnp.bfloat16)
            summed_output = summed_output + lax.optimization_barrier(part).astype(jnp.float32)
        expert_out = lax.optimization_barrier(summed_output.astype(jnp.bfloat16)).astype(jnp.float32)
        carry = carry.at[table].add(weight_tab[:, None] * expert_out, mode='drop')
        return (carry, None)
    start = jnp.zeros((count_tokens, D), jnp.float32)
    moe_sum, unused = lax.scan(one_expert, start, (w_gate, w_up, w_down, jnp.arange(EXPERTS).astype(jnp.int32)))
    layer_out = (mixed_wide + moe_sum).astype(jnp.bfloat16)
    return layer_out.reshape(N_DP, SEQ, D)
```

```python
import functools

import jax
import jax.numpy as jnp
from jax import lax
from jax.experimental import pallas as pl
from jax.experimental.pallas import tpu as pltpu
from jax.sharding import PartitionSpec as P

QH = 32
KVH = 2
HEAD_WIDTH = 128
LANES = 128
DOWN_TILE = 512


def rotate(rows, heads, offset):
    length = rows.shape[0]
    head_size = rows.shape[1] // heads
    values = rows.astype(jnp.float32).reshape(length, heads, head_size)
    half = head_size // 2
    places = (offset + jnp.arange(length)).astype(jnp.float32)
    freqs = jnp.power(
        jnp.float32(1000000.0), -(jnp.arange(half).astype(jnp.float32) * 2.0 / head_size)
    )
    angles = places[:, None] * freqs[None, :]
    cosine = jnp.cos(angles)[:, None, :]
    sine = jnp.sin(angles)[:, None, :]
    first = values[..., :half]
    second = values[..., half:]
    turned = jnp.concatenate(
        [first * cosine - second * sine, second * cosine + first * sine], axis=-1
    )
    return turned.astype(jnp.bfloat16)


def swap(block, axis, bits):
    return lax.ppermute(block, axis, [(i, i ^ bits) for i in range(lax.axis_size(axis))])


def gather_block(block):
    half = block.shape[0] // 2
    along = swap(block, "ctx", 1)
    across = swap(block, "ctx", 2)
    upper = swap(along[:half], "ctx", 2)
    lower = swap(across[half:], "ctx", 1)
    pieces = [jnp.concatenate([block, along, across, upper, lower], axis=0)]
    bits = 1
    while bits < lax.axis_size("tensor"):
        whole = pieces[0] if len(pieces) == 1 else jnp.concatenate(pieces, axis=0)
        pieces.append(swap(whole, "tensor", bits))
        bits *= 2
    return pieces


def add(*terms):
    total = terms[0].astype(jnp.float32)
    for term in terms[1:]:
        total = total + term.astype(jnp.float32)
    return total.astype(jnp.bfloat16)


def sum_block(pieces):
    pieces = list(pieces)
    while len(pieces) > 1:
        last = pieces.pop()
        arrived = swap(last, "tensor", 1 << (len(pieces) - 1))
        start = 0
        for n, piece in enumerate(pieces):
            pieces[n] = add(piece, arrived[start : start + piece.shape[0]])
            start += piece.shape[0]
    rows = pieces[0]
    size = rows.shape[0] // 4
    half = size // 2
    own, along, across = rows[:size], rows[size : 2 * size], rows[2 * size : 3 * size]
    upper = swap(rows[3 * size : 3 * size + half], "ctx", 2)
    lower = swap(rows[3 * size + half :], "ctx", 1)
    along = jnp.concatenate([add(along[:half], upper), along[half:]], axis=0)
    across = jnp.concatenate([across[:half], add(across[half:], lower)], axis=0)
    return add(own, swap(along, "ctx", 1), swap(across, "ctx", 2))


def expert_kernel(count, *refs):
    x_refs, refs = refs[:count], refs[count:]
    mine_ref, gate_ref, up_ref, down_ref = refs[:4]
    y_refs, refs = refs[4 : 4 + count], refs[4 + count :]
    first, second, hidden, first_sem, second_sem = refs
    experts, width, units = gate_ref.shape
    blocks = units // LANES
    tiles = width // DOWN_TILE

    def first_copies(step):
        e, j = step // blocks, step % blocks
        cols = pl.ds(j * LANES, LANES)
        return [
            pltpu.make_async_copy(
                ref.at[e, :, cols], first.at[step, :, pl.ds(side * LANES, LANES)], first_sem.at[step, side]
            )
            for side, ref in enumerate((gate_ref, up_ref))
        ]

    def second_copies(tile):
        cols = pl.ds(tile * DOWN_TILE, DOWN_TILE)
        return [
            pltpu.make_async_copy(
                down_ref.at[e, :, cols], second.at[tile, pl.ds(e * units, units), :], second_sem.at[tile, e]
            )
            for e in range(experts)
        ]

    for step in range(experts * blocks):
        for copy in first_copies(step):
            copy.start()
    for tile in range(tiles):
        for copy in second_copies(tile):
            copy.start()

    for step in range(experts * blocks):
        for copy in first_copies(step):
            copy.wait()
        e = step // blocks
        start = 0
        for x_ref in x_refs:
            rows = x_ref.shape[0]
            weight = jnp.sum(
                x_ref[:, width:].astype(jnp.float32) * mine_ref[e : e + 1, :], axis=1, keepdims=True
            )
            both = jnp.dot(x_ref[:, :width], first[step], preferred_element_type=jnp.float32)
            gate_val, up_val = both[:, :LANES], both[:, LANES:]
            value = gate_val / (1.0 + jnp.exp(-gate_val)) * up_val * weight
            hidden[start : start + rows, step * LANES : (step + 1) * LANES] = value.astype(jnp.bfloat16)
            start += rows

    for tile in range(tiles):
        for copy in second_copies(tile):
            copy.wait()
        start = 0
        for y_ref in y_refs:
            rows = y_ref.shape[0]
            y_ref[:, tile * DOWN_TILE : (tile + 1) * DOWN_TILE] = jnp.dot(
                hidden[start : start + rows], second[tile], preferred_element_type=jnp.float32
            ).astype(jnp.bfloat16)
            start += rows


def expert_block(pieces, mine, w_gate, w_up, w_down):
    experts, width, units = w_gate.shape
    rows = sum(piece.shape[0] for piece in pieces)
    blocks = experts * units // LANES
    vmem = pl.BlockSpec(memory_space=pltpu.VMEM)
    hbm = pl.BlockSpec(memory_space=pl.ANY)
    return pl.pallas_call(
        functools.partial(expert_kernel, len(pieces)),
        out_shape=[jax.ShapeDtypeStruct((piece.shape[0], width), jnp.bfloat16) for piece in pieces],
        in_specs=[vmem] * (len(pieces) + 1) + [hbm] * 3,
        out_specs=[vmem] * len(pieces),
        scratch_shapes=[
            pltpu.VMEM((blocks, width, 2 * LANES), jnp.bfloat16),
            pltpu.VMEM((width // DOWN_TILE, experts * units, DOWN_TILE), jnp.bfloat16),
            pltpu.VMEM((rows, experts * units), jnp.bfloat16),
            pltpu.SemaphoreType.DMA((blocks, 2)),
            pltpu.SemaphoreType.DMA((width // DOWN_TILE, experts)),
        ],
        compiler_params=pltpu.CompilerParams(vmem_limit_bytes=48 * 1024 * 1024),
        cost_estimate=pl.CostEstimate(
            flops=6 * rows * experts * units * width,
            bytes_accessed=6 * experts * units * width + 4 * rows * width,
            transcendentals=rows * experts * units,
        ),
    )(*pieces, mine, w_gate, w_up, w_down)


def on_device(
    query_rows,
    key_rows,
    value_rows,
    residual,
    out_proj,
    post_gain,
    router,
    routes,
    w_gate,
    w_up,
    w_down,
):
    kv_total = KVH
    head_size = HEAD_WIDTH
    local_tokens = query_rows.shape[1]
    local_heads = query_rows.shape[2] // head_size
    group = QH // kv_total
    key_all, value_all = (
        lax.all_gather(key_rows[0], "ctx", axis=0, tiled=True),
        lax.all_gather(value_rows[0], "ctx", axis=0, tiled=True),
    )
    whole = key_all.shape[0]
    offset = lax.axis_index("ctx") * local_tokens
    qrot = rotate(query_rows[0], local_heads, offset)
    krot = rotate(key_all, kv_total, 0)
    head_ids = lax.axis_index("tensor") * local_heads + jnp.arange(local_heads)
    kv_ids = head_ids // group
    key_heads = jnp.take(krot, kv_ids, axis=1)
    value_heads = jnp.take(value_all.reshape(whole, kv_total, head_size), kv_ids, axis=1)
    attention_score = jnp.einsum(
        "qhd,khd->hqk", qrot, key_heads, preferred_element_type=jnp.float32
    ) / jnp.sqrt(jnp.float32(head_size))
    causal = (offset + jnp.arange(local_tokens))[:, None] >= jnp.arange(whole)[None, :]
    attention_score = jnp.where(causal[None], attention_score, jnp.float32(-1e30))
    peak = jnp.max(attention_score, axis=-1, keepdims=True)
    expon = jnp.where(causal[None], jnp.exp(attention_score - peak), jnp.float32(0.0))
    total = jnp.sum(expon, axis=-1)
    softmax_weights = expon.astype(jnp.bfloat16)
    summed_output = jnp.einsum(
        "hqk,khd->qhd", softmax_weights, value_heads, preferred_element_type=jnp.float32
    )
    attended = (
        (summed_output / jnp.transpose(total)[:, :, None])
        .astype(jnp.bfloat16)
        .reshape(local_tokens, local_heads * head_size)
    )
    projected = lax.psum_scatter(
        jnp.dot(attended, out_proj, preferred_element_type=jnp.float32),
        "tensor",
        scatter_dimension=0,
        tiled=True,
    )
    mixed_wide = residual[0].astype(jnp.float32) + projected
    mixed = mixed_wide.astype(jnp.bfloat16)
    mixed_wide = mixed.astype(jnp.float32)
    scale = lax.rsqrt(jnp.mean(mixed_wide * mixed_wide, axis=-1, keepdims=True) + 1e-06)
    normed = (mixed_wide * scale * post_gain.astype(jnp.float32)).astype(jnp.bfloat16)
    logits = jnp.dot(normed, router, preferred_element_type=jnp.float32)
    picks = routes[0]
    tokens = picks.shape[0]
    experts_all = router.shape[1]
    chosen = jnp.any(picks[:, :, None] == jnp.arange(experts_all)[None, None, :], axis=1)
    peak_logit = jnp.max(jnp.where(chosen, logits, -jnp.inf), axis=1, keepdims=True)
    numer = jnp.where(chosen, jnp.exp(jnp.where(chosen, logits - peak_logit, 0.0)), 0.0)
    gates = numer / jnp.sum(numer, axis=1, keepdims=True)
    gates_high = gates.astype(jnp.bfloat16)
    gates_low = (gates - gates_high.astype(jnp.float32)).astype(jnp.bfloat16)
    lanes = -(-2 * experts_all // LANES) * LANES
    spare = jnp.zeros((tokens, lanes - 2 * experts_all), jnp.bfloat16)
    block = jnp.concatenate([normed, gates_high, gates_low, spare], axis=1)

    exp_dev = w_gate.shape[0]
    first = (lax.axis_index("ctx") * lax.axis_size("tensor") + lax.axis_index("tensor")) * exp_dev
    lane = jnp.arange(lanes)
    mine = jnp.stack(
        [(lane == first + e) | (lane == experts_all + first + e) for e in range(exp_dev)]
    ).astype(jnp.float32)

    sums = []
    for bits in range(lax.axis_size("dp")):
        moved = block if bits == 0 else swap(block, "dp", bits)
        sums.append(expert_block(gather_block(moved), mine, w_gate, w_up, w_down))
    moe_sum = jnp.zeros(normed.shape, jnp.float32)
    for bits in reversed(range(lax.axis_size("dp"))):
        part = sum_block(sums[bits])
        moe_sum = moe_sum + (part if bits == 0 else swap(part, "dp", bits)).astype(jnp.float32)
    layer_out = (mixed_wide + moe_sum).astype(jnp.bfloat16)
    return layer_out[None]


def solution(mesh):
    in_specs = (
        P("dp", "ctx", "tensor"),
        P("dp", "ctx", None),
        P("dp", "ctx", None),
        P("dp", ("ctx", "tensor"), None),
        P("tensor", None),
        P(),
        P(),
        P("dp", ("ctx", "tensor"), None),
        P(("ctx", "tensor"), None, "dp"),
        P(("ctx", "tensor"), None, "dp"),
        P(("ctx", "tensor"), "dp", None),
    )
    out_specs = P("dp", ("ctx", "tensor"), None)
    return jax.shard_map(
        on_device, mesh=mesh, in_specs=in_specs, out_specs=out_specs, check_vma=False
    )
```

```python
import functools

import jax
import jax.numpy as jnp
from jax import lax
from jax.experimental import pallas as pl
from jax.experimental.pallas import tpu as pltpu
from jax.sharding import PartitionSpec as P

QH = 32
KVH = 2
HEAD_WIDTH = 128
LANES = 128
DOWN_TILE = 512
UP_VMEM = 26 * 1024 * 1024
DOWN_VMEM = 14 * 1024 * 1024
DOWN_SLOTS = 4


def rotate(rows, places):
    length = rows.shape[0]
    values = rows.astype(jnp.float32).reshape(length, -1, HEAD_WIDTH)
    half = HEAD_WIDTH // 2
    freqs = jnp.power(
        jnp.float32(1000000.0), -(jnp.arange(half).astype(jnp.float32) * 2.0 / HEAD_WIDTH)
    )
    angles = places.astype(jnp.float32)[:, None] * freqs[None, :]
    cosine = jnp.cos(angles)[:, None, :]
    sine = jnp.sin(angles)[:, None, :]
    first = values[..., :half]
    second = values[..., half:]
    turned = jnp.concatenate(
        [first * cosine - second * sine, second * cosine + first * sine], axis=-1
    )
    return turned.astype(jnp.bfloat16)


def swap(block, axis, bits):
    return lax.ppermute(block, axis, [(i, i ^ bits) for i in range(lax.axis_size(axis))])


def add(*terms):
    total = terms[0].astype(jnp.float32)
    for term in terms[1:]:
        total = total + term.astype(jnp.float32)
    return total.astype(jnp.bfloat16)


def exchange(moves, flag):
    *blocks, flag = lax.optimization_barrier((*[move[0] for move in moves], flag))
    return [swap(block, axis, bits) for block, (_, axis, bits) in zip(blocks, moves)], flag


def fence_kernel(flag_ref, *refs):
    refs[-1][...] = flag_ref[...]


def fence(flag, *earlier):
    vmem = pl.BlockSpec(memory_space=pltpu.VMEM)
    hbm = pl.BlockSpec(memory_space=pl.ANY)
    return pl.pallas_call(
        fence_kernel,
        out_shape=jax.ShapeDtypeStruct(flag.shape, flag.dtype),
        in_specs=[vmem] + [hbm] * len(earlier),
        out_specs=vmem,
        cost_estimate=pl.CostEstimate(flops=20_000_000_000, bytes_accessed=0, transcendentals=0),
    )(flag, *earlier)


def fold(rows, size):
    bits = 2
    while bits < size:
        rows = [jnp.concatenate(rows, axis=0)]
        rows = [jnp.concatenate([rows[0], swap(rows[0], "tensor", bits)], axis=0)]
        bits *= 2
    return rows


def unfold(pieces, size):
    bits = size // 2
    while bits > 1:
        half = pieces[0].shape[0] // 2
        pieces = [add(pieces[0][:half], swap(pieces[0][half:], "tensor", bits))]
        bits //= 2
    if len(pieces) > 1:
        return pieces
    rows = pieces[0].shape[0]
    return jnp.split(pieces[0], [rows // 4, rows // 2, rows * 3 // 4, rows * 7 // 8])


def up_kernel(count, later, *refs):
    x_refs, refs = refs[:count], refs[count:]
    mine_ref, refs = refs[0], refs[1 + later :]
    gate_ref, other_gate_ref, up_ref, other_up_ref, refs = *refs[:4], refs[4:]
    hidden_ref, rows_in, weights, rows_sem, weights_sem = refs
    experts, width, units = gate_ref.shape
    row_copies, start = [], 0
    for n, x_ref in enumerate(x_refs):
        rows = x_ref.shape[0]
        row_copies.append(pltpu.make_async_copy(x_ref, rows_in.at[pl.ds(start, rows), :], rows_sem.at[n]))
        start += rows
    weight_copies = [
        [
            pltpu.make_async_copy(
                ref.at[e], weights.at[e, :, pl.ds(side * units, units)], weights_sem.at[e, side]
            )
            for side, ref in enumerate((other_gate_ref, other_up_ref))
        ]
        for e in range(experts)
    ]
    for copies in [row_copies] + weight_copies:
        for copy in copies:
            copy.start()
    for copy in row_copies:
        copy.wait()

    def store(e, gate_val, up_val):
        spare = rows_in[:, width:].astype(jnp.float32)
        weight = jnp.sum(spare * mine_ref[e : e + 1, :], axis=1, keepdims=True)
        value = gate_val / (1.0 + jnp.exp(-gate_val)) * up_val * weight
        hidden_ref[:, e * units : (e + 1) * units] = value.astype(jnp.bfloat16)

    def times(mat):
        return jnp.dot(rows_in[:, :width], mat, preferred_element_type=jnp.float32)

    for e in range(experts):
        even = units // (2 * LANES) * 2 * LANES
        both = times(jnp.concatenate([gate_ref[e, :, even:], up_ref[e, :, even:]], axis=1))
        store(
            e,
            jnp.concatenate([times(gate_ref[e, :, :even]), both[:, : units - even]], axis=1),
            jnp.concatenate([times(up_ref[e, :, :even]), both[:, units - even :]], axis=1),
        )
    for e in range(experts):
        for copy in weight_copies[e]:
            copy.wait()
        both = times(weights[e])
        store(experts + e, both[:, :units], both[:, units:])


def up_block(pieces, mine, later, gates, ups):
    experts, width, units = gates[0].shape
    rows = sum(piece.shape[0] for piece in pieces)
    vmem = pl.BlockSpec(memory_space=pltpu.VMEM)
    hbm = pl.BlockSpec(memory_space=pl.ANY)
    return pl.pallas_call(
        functools.partial(up_kernel, len(pieces), len(later)),
        out_shape=jax.ShapeDtypeStruct((rows, 2 * experts * units), jnp.bfloat16),
        in_specs=[hbm] * len(pieces) + [vmem] + [hbm] * len(later) + [vmem, hbm] * 2,
        out_specs=vmem,
        scratch_shapes=[
            pltpu.VMEM((rows, pieces[0].shape[1]), jnp.bfloat16),
            pltpu.VMEM((experts, width, 2 * units), jnp.bfloat16),
            pltpu.SemaphoreType.DMA((len(pieces),)),
            pltpu.SemaphoreType.DMA((experts, 2)),
        ],
        compiler_params=pltpu.CompilerParams(vmem_limit_bytes=UP_VMEM),
        cost_estimate=pl.CostEstimate(
            flops=8 * rows * experts * units * width,
            bytes_accessed=8 * experts * units * width + 2 * rows * width,
            transcendentals=2 * rows * experts * units,
        ),
    )(*pieces, mine, *later, *gates, *ups)


def down_kernel(count, later, hidden_ref, *refs):
    down_refs, refs = refs[later : later + 2], refs[later + 2 :]
    y_refs, (weights, weights_sem) = refs[:count], refs[count:]
    experts, units, width = down_refs[0].shape
    tiles = width // DOWN_TILE
    copies = [
        [
            pltpu.make_async_copy(
                down_refs[e // experts].at[e % experts, :, pl.ds(tile * DOWN_TILE, DOWN_TILE)],
                weights.at[tile % DOWN_SLOTS, pl.ds(e * units, units), :],
                weights_sem.at[tile % DOWN_SLOTS, e],
            )
            for e in range(2 * experts)
        ]
        for tile in range(tiles)
    ]
    for group in copies[: DOWN_SLOTS - 1]:
        for copy in group:
            copy.start()
    for tile in range(tiles):
        for group in copies[tile + DOWN_SLOTS - 1 : tile + DOWN_SLOTS]:
            for copy in group:
                copy.start()
        for copy in copies[tile]:
            copy.wait()
        cols = slice(tile * DOWN_TILE, (tile + 1) * DOWN_TILE)
        result = jnp.dot(
            hidden_ref[...], weights[tile % DOWN_SLOTS], preferred_element_type=jnp.float32
        ).astype(jnp.bfloat16)
        start = 0
        for y_ref in y_refs:
            rows = y_ref.shape[0]
            y_ref[:, cols] = result[start : start + rows]
            start += rows


def down_block(hidden, sizes, later, downs):
    experts, units, width = downs[0].shape
    rows = hidden.shape[0]
    vmem = pl.BlockSpec(memory_space=pltpu.VMEM)
    hbm = pl.BlockSpec(memory_space=pl.ANY)
    return pl.pallas_call(
        functools.partial(down_kernel, len(sizes), len(later)),
        out_shape=[jax.ShapeDtypeStruct((size, width), jnp.bfloat16) for size in sizes],
        in_specs=[vmem] + [hbm] * (len(later) + 2),
        out_specs=[vmem] * len(sizes),
        scratch_shapes=[
            pltpu.VMEM((DOWN_SLOTS, 2 * experts * units, DOWN_TILE), jnp.bfloat16),
            pltpu.SemaphoreType.DMA((DOWN_SLOTS, 2 * experts)),
        ],
        compiler_params=pltpu.CompilerParams(vmem_limit_bytes=DOWN_VMEM),
        cost_estimate=pl.CostEstimate(
            flops=4 * rows * experts * units * width,
            bytes_accessed=4 * experts * units * width + 2 * rows * width,
            transcendentals=0,
        ),
    )(hidden, *later, *downs)


def on_device(
    query_rows,
    key_rows,
    value_rows,
    residual,
    out_proj,
    post_gain,
    router,
    routes,
    w_gate,
    w_up,
    w_down,
):
    gates_pair, ups_pair = [(w, swap(w, "tensor", 1)) for w in (w_gate, w_up)]
    local_tokens = query_rows.shape[1]
    local_heads = query_rows.shape[2] // HEAD_WIDTH
    group = QH // KVH
    kv_dev = max(1, local_heads // group)
    share = local_heads // kv_dev
    kv_first = lax.axis_index("tensor") * local_heads // group * HEAD_WIDTH
    my_ctx = lax.axis_index("ctx")
    pair = jnp.concatenate(
        [
            lax.dynamic_slice_in_dim(rows[0], kv_first, kv_dev * HEAD_WIDTH, axis=1)
            for rows in (key_rows, value_rows)
        ],
        axis=1,
    )
    contexts = lax.axis_size("ctx")
    pairs = jnp.concatenate([pair] + [swap(pair, "ctx", bits) for bits in range(1, contexts)], axis=0)
    within = jnp.arange(local_tokens)
    places = my_ctx * local_tokens + within
    key_places = jnp.concatenate([(my_ctx ^ bits) * local_tokens + within for bits in range(contexts)])
    qrot = rotate(query_rows[0], places).reshape(local_tokens, kv_dev, share, HEAD_WIDTH)
    krot = rotate(pairs[:, : kv_dev * HEAD_WIDTH], key_places)
    value_heads = pairs[:, kv_dev * HEAD_WIDTH :].reshape(-1, kv_dev, HEAD_WIDTH)
    attention_score = jnp.einsum(
        "qghd,kgd->ghqk", qrot, krot, preferred_element_type=jnp.float32
    ) / jnp.sqrt(jnp.float32(HEAD_WIDTH))
    causal = places[:, None] >= key_places[None, :]
    attention_score = jnp.where(causal, attention_score, jnp.float32(-1e30))
    peak = jnp.max(attention_score, axis=-1, keepdims=True)
    expon = jnp.where(causal, jnp.exp(attention_score - peak), jnp.float32(0.0))
    total = jnp.sum(expon, axis=-1)
    softmax_weights = expon.astype(jnp.bfloat16)
    summed_output = jnp.einsum(
        "ghqk,kgd->qghd", softmax_weights, value_heads, preferred_element_type=jnp.float32
    )
    attended = (
        (summed_output / jnp.transpose(total, (2, 0, 1))[..., None])
        .astype(jnp.bfloat16)
        .reshape(local_tokens, local_heads * HEAD_WIDTH)
    )
    projected = jnp.dot(attended, out_proj, preferred_element_type=jnp.float32)
    bits = lax.axis_size("tensor") // 2
    while bits:
        half = projected.shape[0] // 2
        high = (lax.axis_index("tensor") & bits) != 0
        keep = jnp.where(high, projected[half:], projected[:half])
        give = jnp.where(high, projected[:half], projected[half:])
        projected = keep + swap(give, "tensor", bits)
        bits //= 2
    mixed_wide = residual[0].astype(jnp.float32) + projected
    mixed = mixed_wide.astype(jnp.bfloat16)
    mixed, w_down = lax.optimization_barrier((mixed, w_down))
    downs_pair = w_down, swap(w_down, "tensor", 1)
    mixed_wide = mixed.astype(jnp.float32)
    scale = lax.rsqrt(jnp.mean(mixed_wide * mixed_wide, axis=-1, keepdims=True) + 1e-06)
    normed = (mixed_wide * scale * post_gain.astype(jnp.float32)).astype(jnp.bfloat16)
    logits = jnp.dot(normed, router, preferred_element_type=jnp.float32)
    picks = routes[0]
    tokens = picks.shape[0]
    experts_all = router.shape[1]
    chosen = jnp.any(picks[:, :, None] == jnp.arange(experts_all)[None, None, :], axis=1)
    peak_logit = jnp.max(jnp.where(chosen, logits, -jnp.inf), axis=1, keepdims=True)
    numer = jnp.where(chosen, jnp.exp(jnp.where(chosen, logits - peak_logit, 0.0)), 0.0)
    gates = numer / jnp.sum(numer, axis=1, keepdims=True)
    gates_high = gates.astype(jnp.bfloat16)
    gates_low = (gates - gates_high.astype(jnp.float32)).astype(jnp.bfloat16)
    lanes = -(-2 * experts_all // LANES) * LANES
    spare = jnp.zeros((tokens, lanes - 2 * experts_all), jnp.bfloat16)
    block = jnp.concatenate([normed, gates_high, gates_low, spare], axis=1)

    exp_dev = w_gate.shape[0]
    lane = jnp.arange(lanes)
    mine = []
    for core in (0, 1):
        group_id = lax.axis_index("ctx") * lax.axis_size("tensor") + (lax.axis_index("tensor") ^ core)
        for e in range(exp_dev):
            expert = group_id * exp_dev + e
            mine.append((lane == expert) | (lane == experts_all + expert))
    mine = jnp.stack(mine).astype(jnp.float32)

    cores = lax.axis_size("tensor")
    middle = tokens // 2

    def out_near(rows):
        return [(rows, "ctx", 1), (rows, "ctx", 2)]

    def out_corner(near):
        return [(near[0][:middle], "ctx", 2), (near[1][middle:], "ctx", 1)]

    def back_corner(sums):
        return [(sums[3], "ctx", 2), (sums[4], "ctx", 1)]

    def back_near(sums, corner):
        first = jnp.concatenate([add(sums[1][:middle], corner[0]), sums[1][middle:]], axis=0)
        second = jnp.concatenate([sums[2][:middle], add(sums[2][middle:], corner[1])], axis=0)
        return [(first, "ctx", 1), (second, "ctx", 2)]

    def up_of(own, near, corner, flag):
        pieces = fold([own, *near, *corner], cores)
        return up_block(pieces, flag, [], gates_pair, ups_pair), [piece.shape[0] for piece in pieces]

    def down_of(hidden, later):
        return unfold(down_block(*hidden, later, downs_pair), cores)

    block, *arrived = lax.optimization_barrier((block, gates_pair[1], ups_pair[1]))
    gates_pair, ups_pair = (gates_pair[0], arrived[0]), (ups_pair[0], arrived[1])
    flag = fence(mine, block)
    (*near0, rows1), mine = exchange([*out_near(block), (block, "dp", 1)], mine)
    (*got, rows2), flag = exchange([*out_corner(near0), *out_near(rows1), (block, "dp", 2)], flag)
    corner0, near1 = got[:2], got[2:]
    flag = fence(flag, *near0, rows1)
    (*got, rows3), flag = exchange([*out_corner(near1), *out_near(rows2), (block, "dp", 3)], flag)
    corner1, near2 = got[:2], got[2:]
    hidden0 = up_of(block, near0, corner0, flag)
    got, _ = exchange([*out_corner(near2), *out_near(rows3)], hidden0[0])
    corner2, near3 = got[:2], got[2:]
    sums0 = down_of(hidden0, [*corner1, *near2, rows3])
    hidden1 = up_of(rows1, near1, corner1, flag)
    got, _ = exchange([*out_corner(near3), *back_corner(sums0)], hidden1[0])
    corner3, half0 = got[:2], got[2:]
    sums1 = down_of(hidden1, [*corner2, *near3])
    hidden2 = up_of(rows2, near2, corner2, flag)
    got, _ = exchange([*back_corner(sums1), *back_near(sums0, half0)], hidden2[0])
    half1, full0 = got[:2], got[2:]
    sums2 = down_of(hidden2, [*corner3, *half0])
    half2, _ = exchange(back_corner(sums2), flag)
    hidden3 = up_of(rows3, near3, corner3, flag)
    full1, _ = exchange(back_near(sums1, half1), flag)
    full2, _ = exchange(back_near(sums2, half2), hidden3[0])
    sums3 = down_of(hidden3, [*half2, *full1])
    half3, _ = exchange(back_corner(sums3), flag)
    total1, total2 = add(sums1[0], *full1), add(sums2[0], *full2)
    (part1, part2), _ = exchange([(total1, "dp", 1), (total2, "dp", 2)], flag)
    full3, _ = exchange(back_near(sums3, half3), flag)
    total3 = add(sums3[0], *full3)
    part3 = swap(total3, "dp", 3)
    moe_sum = sums0[0].astype(jnp.float32)
    for part in (*full0, part1, part2, part3):
        moe_sum = moe_sum + part.astype(jnp.float32)
    layer_out = (mixed_wide + moe_sum).astype(jnp.bfloat16)
    return layer_out[None]


def solution(mesh):
    in_specs = (
        P("dp", "ctx", "tensor"),
        P("dp", "ctx", None),
        P("dp", "ctx", None),
        P("dp", ("ctx", "tensor"), None),
        P("tensor", None),
        P(),
        P(),
        P("dp", ("ctx", "tensor"), None),
        P(("ctx", "tensor"), None, "dp"),
        P(("ctx", "tensor"), None, "dp"),
        P(("ctx", "tensor"), "dp", None),
    )
    out_specs = P("dp", ("ctx", "tensor"), None)
    return jax.shard_map(
        on_device, mesh=mesh, in_specs=in_specs, out_specs=out_specs, check_vma=False
    )
```

```python
import functools

import jax
import jax.numpy as jnp
from jax import lax
from jax.experimental import pallas as pl
from jax.experimental.pallas import tpu as pltpu
from jax.sharding import PartitionSpec as P

QH = 32
KVH = 2
HEAD_WIDTH = 128
LANES = 128
DOWN_TILE = 512
UP_VMEM = 30 * 1024 * 1024
UP_SLOTS = 3
UP_PARTS = 4
SMALL_VMEM = 4 * 1024 * 1024
DOWN_VMEM = 14 * 1024 * 1024
DOWN_SLOTS = 4


def rotate(rows, places):
    length = rows.shape[0]
    values = rows.astype(jnp.float32).reshape(length, -1, HEAD_WIDTH)
    half = HEAD_WIDTH // 2
    freqs = jnp.power(
        jnp.float32(1000000.0), -(jnp.arange(half).astype(jnp.float32) * 2.0 / HEAD_WIDTH)
    )
    angles = places.astype(jnp.float32)[:, None] * freqs[None, :]
    cosine = jnp.cos(angles)[:, None, :]
    sine = jnp.sin(angles)[:, None, :]
    first = values[..., :half]
    second = values[..., half:]
    turned = jnp.concatenate(
        [first * cosine - second * sine, second * cosine + first * sine], axis=-1
    )
    return turned.astype(jnp.bfloat16)


def swap(block, axis, bits):
    return lax.ppermute(block, axis, [(i, i ^ bits) for i in range(lax.axis_size(axis))])


def add(*terms):
    total = terms[0].astype(jnp.float32)
    for term in terms[1:]:
        total = total + term.astype(jnp.float32)
    return total.astype(jnp.bfloat16)


def exchange(moves, flag):
    *blocks, flag = lax.optimization_barrier((*[move[0] for move in moves], flag))
    return [swap(block, axis, bits) for block, (_, axis, bits) in zip(blocks, moves)], flag


def fence_kernel(flag_ref, *refs):
    refs[-1][...] = flag_ref[...]


def fence(flag, earlier, resident=()):
    vmem = pl.BlockSpec(memory_space=pltpu.VMEM)
    hbm = pl.BlockSpec(memory_space=pl.ANY)
    return pl.pallas_call(
        fence_kernel,
        out_shape=jax.ShapeDtypeStruct(flag.shape, flag.dtype),
        in_specs=[vmem] + [hbm] * len(earlier) + [vmem] * len(resident),
        out_specs=vmem,
        compiler_params=pltpu.CompilerParams(vmem_limit_bytes=UP_VMEM if resident else SMALL_VMEM),
        cost_estimate=pl.CostEstimate(flops=20_000_000_000, bytes_accessed=0, transcendentals=0),
    )(flag, *earlier, *resident)


def halves_kernel(first_ref, second_ref, upper_ref, lower_ref):
    middle = upper_ref.shape[0]
    upper_ref[...] = first_ref[:middle]
    lower_ref[...] = second_ref[middle:]


def halves(first, second):
    rows, width = first.shape
    vmem = pl.BlockSpec(memory_space=pltpu.VMEM)
    shape = jax.ShapeDtypeStruct((rows // 2, width), first.dtype)
    return pl.pallas_call(
        halves_kernel,
        out_shape=[shape] * 2,
        in_specs=[vmem] * 2,
        out_specs=[vmem] * 2,
        compiler_params=pltpu.CompilerParams(vmem_limit_bytes=SMALL_VMEM),
    )(first, second)


def join_kernel(first_ref, second_ref, upper_ref, lower_ref, one_ref, other_ref):
    middle = upper_ref.shape[0]

    def plus(rows, more):
        return (rows.astype(jnp.float32) + more.astype(jnp.float32)).astype(jnp.bfloat16)

    one_ref[:middle] = plus(first_ref[:middle], upper_ref[...])
    one_ref[middle:] = first_ref[middle:]
    other_ref[:middle] = second_ref[:middle]
    other_ref[middle:] = plus(second_ref[middle:], lower_ref[...])


def join(first, second, upper, lower):
    vmem = pl.BlockSpec(memory_space=pltpu.VMEM)
    shape = jax.ShapeDtypeStruct(first.shape, first.dtype)
    return pl.pallas_call(
        join_kernel,
        out_shape=[shape] * 2,
        in_specs=[vmem] * 4,
        out_specs=[vmem] * 2,
        compiler_params=pltpu.CompilerParams(vmem_limit_bytes=SMALL_VMEM),
    )(first, second, upper, lower)


def fold(rows, size):
    bits = 2
    while bits < size:
        rows = [jnp.concatenate(rows, axis=0)]
        rows = [jnp.concatenate([rows[0], swap(rows[0], "tensor", bits)], axis=0)]
        bits *= 2
    return rows


def unfold(pieces, size):
    bits = size // 2
    while bits > 1:
        half = pieces[0].shape[0] // 2
        pieces = [add(pieces[0][:half], swap(pieces[0][half:], "tensor", bits))]
        bits //= 2
    if len(pieces) > 1:
        return pieces
    rows = pieces[0].shape[0]
    return jnp.split(pieces[0], [rows // 4, rows // 2, rows * 3 // 4, rows * 7 // 8])


def up_kernel(count, later, *refs):
    x_refs, refs = refs[:count], refs[count:]
    mine_ref, refs = refs[0], refs[1 + later :]
    gate_refs, up_refs, refs = refs[0:2], refs[2:4], refs[4:]
    hidden_ref, rows_in, weights, rows_sem, weights_sem = refs
    experts, width, units = gate_refs[0].shape
    row_copies, start = [], 0
    for n, x_ref in enumerate(x_refs):
        rows = x_ref.shape[0]
        row_copies.append(pltpu.make_async_copy(x_ref, rows_in.at[pl.ds(start, rows), :], rows_sem.at[n]))
        start += rows

    def parts_of(e):
        return UP_PARTS if e == 0 else 1

    def weight_copies(e, part):
        size = width // parts_of(e)
        span = pl.ds(part * size, size)
        return [
            pltpu.make_async_copy(
                ref.at[e % experts, span, :],
                weights.at[e % UP_SLOTS, span, pl.ds(side * units, units)],
                weights_sem.at[e % UP_SLOTS, part, side],
            )
            for side, ref in enumerate((gate_refs[e // experts], up_refs[e // experts]))
        ]

    def start_weights(e):
        if e < 2 * experts:
            for part in range(parts_of(e)):
                for copy in weight_copies(e, part):
                    copy.start()

    for copy in row_copies:
        copy.start()
    for e in range(UP_SLOTS - 1):
        start_weights(e)
    for copy in row_copies:
        copy.wait()
    for e in range(2 * experts):
        start_weights(e + UP_SLOTS - 1)
        both = None
        for part in range(parts_of(e)):
            for copy in weight_copies(e, part):
                copy.wait()
            size = width // parts_of(e)
            span = slice(part * size, (part + 1) * size)
            term = jnp.dot(rows_in[:, span], weights[e % UP_SLOTS, span], preferred_element_type=jnp.float32)
            both = term if both is None else both + term
        gate_val, up_val = both[:, :units], both[:, units:]
        spare = rows_in[:, width:].astype(jnp.float32)
        weight = jnp.sum(spare * mine_ref[e : e + 1, :], axis=1, keepdims=True)
        value = gate_val / (1.0 + jnp.exp(-gate_val)) * up_val * weight
        hidden_ref[:, e * units : (e + 1) * units] = value.astype(jnp.bfloat16)


def up_block(pieces, mine, later, gates, ups):
    experts, width, units = gates[0].shape
    rows = sum(piece.shape[0] for piece in pieces)
    vmem = pl.BlockSpec(memory_space=pltpu.VMEM)
    hbm = pl.BlockSpec(memory_space=pl.ANY)
    return pl.pallas_call(
        functools.partial(up_kernel, len(pieces), len(later)),
        out_shape=jax.ShapeDtypeStruct((rows, 2 * experts * units), jnp.bfloat16),
        in_specs=[hbm] * len(pieces) + [vmem] + [hbm] * (len(later) + 4),
        out_specs=vmem,
        scratch_shapes=[
            pltpu.VMEM((rows, pieces[0].shape[1]), jnp.bfloat16),
            pltpu.VMEM((UP_SLOTS, width, 2 * units), jnp.bfloat16),
            pltpu.SemaphoreType.DMA((len(pieces),)),
            pltpu.SemaphoreType.DMA((UP_SLOTS, UP_PARTS, 2)),
        ],
        compiler_params=pltpu.CompilerParams(vmem_limit_bytes=UP_VMEM),
        cost_estimate=pl.CostEstimate(
            flops=8 * rows * experts * units * width,
            bytes_accessed=8 * experts * units * width + 2 * rows * width,
            transcendentals=2 * rows * experts * units,
        ),
    )(*pieces, mine, *later, *gates, *ups)


def down_kernel(count, later, hidden_ref, *refs):
    down_refs, refs = refs[later : later + 2], refs[later + 2 :]
    y_refs, (weights, weights_sem) = refs[:count], refs[count:]
    experts, units, width = down_refs[0].shape
    tiles = width // DOWN_TILE
    copies = [
        [
            pltpu.make_async_copy(
                down_refs[e // experts].at[e % experts, :, pl.ds(tile * DOWN_TILE, DOWN_TILE)],
                weights.at[tile % DOWN_SLOTS, pl.ds(e * units, units), :],
                weights_sem.at[tile % DOWN_SLOTS, e],
            )
            for e in range(2 * experts)
        ]
        for tile in range(tiles)
    ]
    for group in copies[: DOWN_SLOTS - 1]:
        for copy in group:
            copy.start()
    for tile in range(tiles):
        for group in copies[tile + DOWN_SLOTS - 1 : tile + DOWN_SLOTS]:
            for copy in group:
                copy.start()
        for copy in copies[tile]:
            copy.wait()
        cols = slice(tile * DOWN_TILE, (tile + 1) * DOWN_TILE)
        result = jnp.dot(
            hidden_ref[...], weights[tile % DOWN_SLOTS], preferred_element_type=jnp.float32
        ).astype(jnp.bfloat16)
        start = 0
        for y_ref in y_refs:
            rows = y_ref.shape[0]
            y_ref[:, cols] = result[start : start + rows]
            start += rows


def down_block(hidden, sizes, later, downs):
    experts, units, width = downs[0].shape
    rows = hidden.shape[0]
    vmem = pl.BlockSpec(memory_space=pltpu.VMEM)
    hbm = pl.BlockSpec(memory_space=pl.ANY)
    return pl.pallas_call(
        functools.partial(down_kernel, len(sizes), len(later)),
        out_shape=[jax.ShapeDtypeStruct((size, width), jnp.bfloat16) for size in sizes],
        in_specs=[vmem] + [hbm] * (len(later) + 2),
        out_specs=[vmem] * len(sizes),
        scratch_shapes=[
            pltpu.VMEM((DOWN_SLOTS, 2 * experts * units, DOWN_TILE), jnp.bfloat16),
            pltpu.SemaphoreType.DMA((DOWN_SLOTS, 2 * experts)),
        ],
        compiler_params=pltpu.CompilerParams(vmem_limit_bytes=DOWN_VMEM),
        cost_estimate=pl.CostEstimate(
            flops=4 * rows * experts * units * width,
            bytes_accessed=4 * experts * units * width + 2 * rows * width,
            transcendentals=0,
        ),
    )(hidden, *later, *downs)


def on_device(
    query_rows,
    key_rows,
    value_rows,
    residual,
    out_proj,
    post_gain,
    router,
    routes,
    w_gate,
    w_up,
    w_down,
):
    gates_pair, ups_pair = [(w, swap(w, "tensor", 1)) for w in (w_gate, w_up)]
    local_tokens = query_rows.shape[1]
    local_heads = query_rows.shape[2] // HEAD_WIDTH
    group = QH // KVH
    kv_dev = max(1, local_heads // group)
    share = local_heads // kv_dev
    kv_first = lax.axis_index("tensor") * local_heads // group * HEAD_WIDTH
    my_ctx = lax.axis_index("ctx")
    pair = jnp.concatenate(
        [
            lax.dynamic_slice_in_dim(rows[0], kv_first, kv_dev * HEAD_WIDTH, axis=1)
            for rows in (key_rows, value_rows)
        ],
        axis=1,
    )
    contexts = lax.axis_size("ctx")
    pairs = jnp.concatenate([pair] + [swap(pair, "ctx", bits) for bits in range(1, contexts)], axis=0)
    within = jnp.arange(local_tokens)
    places = my_ctx * local_tokens + within
    key_places = jnp.concatenate([(my_ctx ^ bits) * local_tokens + within for bits in range(contexts)])
    qrot = rotate(query_rows[0], places).reshape(local_tokens, kv_dev, share, HEAD_WIDTH)
    krot = rotate(pairs[:, : kv_dev * HEAD_WIDTH], key_places)
    value_heads = pairs[:, kv_dev * HEAD_WIDTH :].reshape(-1, kv_dev, HEAD_WIDTH)
    attention_score = jnp.einsum(
        "qghd,kgd->ghqk", qrot, krot, preferred_element_type=jnp.float32
    ) / jnp.sqrt(jnp.float32(HEAD_WIDTH))
    causal = places[:, None] >= key_places[None, :]
    attention_score = jnp.where(causal, attention_score, jnp.float32(-1e30))
    peak = jnp.max(attention_score, axis=-1, keepdims=True)
    expon = jnp.where(causal, jnp.exp(attention_score - peak), jnp.float32(0.0))
    total = jnp.sum(expon, axis=-1)
    softmax_weights = expon.astype(jnp.bfloat16)
    summed_output = jnp.einsum(
        "ghqk,kgd->qghd", softmax_weights, value_heads, preferred_element_type=jnp.float32
    )
    attended = (
        (summed_output / jnp.transpose(total, (2, 0, 1))[..., None])
        .astype(jnp.bfloat16)
        .reshape(local_tokens, local_heads * HEAD_WIDTH)
    )
    projected = jnp.dot(attended, out_proj, preferred_element_type=jnp.float32)
    bits = lax.axis_size("tensor") // 2
    while bits:
        half = projected.shape[0] // 2
        high = (lax.axis_index("tensor") & bits) != 0
        keep = jnp.where(high, projected[half:], projected[:half])
        give = jnp.where(high, projected[:half], projected[half:])
        projected = keep + swap(give, "tensor", bits)
        bits //= 2
    mixed_wide = residual[0].astype(jnp.float32) + projected
    mixed = mixed_wide.astype(jnp.bfloat16)
    mixed, w_down = lax.optimization_barrier((mixed, w_down))
    downs_pair = w_down, swap(w_down, "tensor", 1)
    mixed_wide = mixed.astype(jnp.float32)
    scale = lax.rsqrt(jnp.mean(mixed_wide * mixed_wide, axis=-1, keepdims=True) + 1e-06)
    normed = (mixed_wide * scale * post_gain.astype(jnp.float32)).astype(jnp.bfloat16)
    logits = jnp.dot(normed, router, preferred_element_type=jnp.float32)
    picks = routes[0]
    tokens = picks.shape[0]
    experts_all = router.shape[1]
    chosen = jnp.any(picks[:, :, None] == jnp.arange(experts_all)[None, None, :], axis=1)
    peak_logit = jnp.max(jnp.where(chosen, logits, -jnp.inf), axis=1, keepdims=True)
    numer = jnp.where(chosen, jnp.exp(jnp.where(chosen, logits - peak_logit, 0.0)), 0.0)
    gates = numer / jnp.sum(numer, axis=1, keepdims=True)
    gates_high = gates.astype(jnp.bfloat16)
    gates_low = (gates - gates_high.astype(jnp.float32)).astype(jnp.bfloat16)
    lanes = -(-2 * experts_all // LANES) * LANES
    spare = jnp.zeros((tokens, lanes - 2 * experts_all), jnp.bfloat16)
    block = jnp.concatenate([normed, gates_high, gates_low, spare], axis=1)

    exp_dev = w_gate.shape[0]
    lane = jnp.arange(lanes)
    mine = []
    for core in (0, 1):
        group_id = lax.axis_index("ctx") * lax.axis_size("tensor") + (lax.axis_index("tensor") ^ core)
        for e in range(exp_dev):
            expert = group_id * exp_dev + e
            mine.append((lane == expert) | (lane == experts_all + expert))
    mine = jnp.stack(mine).astype(jnp.float32)

    cores = lax.axis_size("tensor")

    def out_near(rows):
        return [(rows, "ctx", 1), (rows, "ctx", 2)]

    def out_corner(near):
        upper, lower = halves(*near)
        return [(upper, "ctx", 2), (lower, "ctx", 1)]

    def back_corner(sums):
        return [(sums[3], "ctx", 2), (sums[4], "ctx", 1)]

    def back_near(sums, corner):
        first, second = join(sums[1], sums[2], *corner)
        return [(first, "ctx", 1), (second, "ctx", 2)]

    def up_of(own, near, corner, later=()):
        pieces = fold([own, *near, *corner], cores)
        return up_block(pieces, flag, later, gates_pair, ups_pair), [piece.shape[0] for piece in pieces]

    def down_of(hidden, later):
        return unfold(down_block(*hidden, later, downs_pair), cores)

    block, *arrived = lax.optimization_barrier((block, gates_pair[1], ups_pair[1]))
    gates_pair, ups_pair = (gates_pair[0], arrived[0]), (ups_pair[0], arrived[1])
    flag = fence(mine, [block])
    (*near0, rows1), mine = exchange([*out_near(block), (block, "dp", 1)], mine)
    flag, other_down = lax.optimization_barrier((flag, downs_pair[1]))
    downs_pair = downs_pair[0], other_down
    (*got, rows2), flag = exchange([*out_corner(near0), *out_near(rows1), (block, "dp", 2)], flag)
    corner0, near1 = got[:2], got[2:]
    flag = fence(flag, [*near0, rows1])
    (*got, rows3), flag = exchange([*out_corner(near1), *out_near(rows2), (block, "dp", 3)], flag)
    corner1, near2 = got[:2], got[2:]
    hidden0 = up_of(block, near0, corner0)
    got, _ = exchange([*out_corner(near2), *out_near(rows3)], hidden0[0])
    corner2, near3 = got[:2], got[2:]
    sums0 = down_of(hidden0, [*corner1, *near2, rows3])
    hidden1 = up_of(rows1, near1, corner1, [sums0[0]])
    got, _ = exchange([*out_corner(near3), *back_corner(sums0)], hidden1[0])
    corner3, half0 = got[:2], got[2:]
    sums1 = down_of(hidden1, [*corner2, *near3])
    hidden2 = up_of(rows2, near2, corner2, [sums1[0]])
    got, _ = exchange([*back_corner(sums1), *back_near(sums0, half0)], hidden2[0])
    half1, full0 = got[:2], got[2:]
    sums2 = down_of(hidden2, [*corner3, *half0])
    half2, _ = exchange(back_corner(sums2), flag)
    hidden3 = up_of(rows3, near3, corner3, [sums2[0]])
    full1, _ = exchange(back_near(sums1, half1), flag)
    full2, _ = exchange(back_near(sums2, half2), hidden3[0])
    sums3 = down_of(hidden3, [*half2, *full1, *full0])
    part1 = swap(add(sums1[0], *full1), "dp", 1)
    part2 = swap(add(sums2[0], *full2), "dp", 2)
    half3, _ = exchange(back_corner(sums3), flag)
    full3, _ = exchange(back_near(sums3, half3), flag)
    part3 = swap(add(sums3[0], *full3), "dp", 3)
    moe_sum = sums0[0].astype(jnp.float32)
    for part in (*full0, part1, part2, part3):
        moe_sum = moe_sum + part.astype(jnp.float32)
    layer_out = (mixed_wide + moe_sum).astype(jnp.bfloat16)
    return layer_out[None]


def solution(mesh):
    in_specs = (
        P("dp", "ctx", "tensor"),
        P("dp", "ctx", None),
        P("dp", "ctx", None),
        P("dp", ("ctx", "tensor"), None),
        P("tensor", None),
        P(),
        P(),
        P("dp", ("ctx", "tensor"), None),
        P(("ctx", "tensor"), None, "dp"),
        P(("ctx", "tensor"), None, "dp"),
        P(("ctx", "tensor"), "dp", None),
    )
    out_specs = P("dp", ("ctx", "tensor"), None)
    return jax.shard_map(
        on_device, mesh=mesh, in_specs=in_specs, out_specs=out_specs, check_vma=False
    )
```

```python
import functools

import jax
import jax.numpy as jnp
from jax import lax
from jax.experimental import pallas as pl
from jax.experimental.pallas import tpu as pltpu
from jax.sharding import PartitionSpec as P

QH = 32
KVH = 2
HEAD_WIDTH = 128
LANES = 128
DOWN_TILE = 512
UP_VMEM = 36 * 1024 * 1024
UP_SLOTS = 3
GROUP = 256
UP_PARTS = 4
SMALL_VMEM = 4 * 1024 * 1024
DOWN_VMEM = 20 * 1024 * 1024


def rotate(rows, places):
    length = rows.shape[0]
    values = rows.astype(jnp.float32).reshape(length, -1, HEAD_WIDTH)
    half = HEAD_WIDTH // 2
    freqs = jnp.power(
        jnp.float32(1000000.0), -(jnp.arange(half).astype(jnp.float32) * 2.0 / HEAD_WIDTH)
    )
    angles = places.astype(jnp.float32)[:, None] * freqs[None, :]
    cosine = jnp.cos(angles)[:, None, :]
    sine = jnp.sin(angles)[:, None, :]
    first = values[..., :half]
    second = values[..., half:]
    turned = jnp.concatenate(
        [first * cosine - second * sine, second * cosine + first * sine], axis=-1
    )
    return turned.astype(jnp.bfloat16)


def swap(block, axis, bits):
    pairs = [(i, i ^ bits) for i in range(lax.axis_size(axis))] if isinstance(bits, int) else bits
    return lax.ppermute(block, axis, pairs)


def add(*terms):
    total = terms[0].astype(jnp.float32)
    for term in terms[1:]:
        total = total + term.astype(jnp.float32)
    return total.astype(jnp.bfloat16)


def exchange(moves, flag):
    *blocks, flag = lax.optimization_barrier((*[move[0] for move in moves], flag))
    return [swap(block, axis, bits) for block, (_, axis, bits) in zip(blocks, moves)], flag


def fence_kernel(flag_ref, *refs):
    refs[-1][...] = flag_ref[...]


def fence(flag, earlier, resident=()):
    vmem = pl.BlockSpec(memory_space=pltpu.VMEM)
    hbm = pl.BlockSpec(memory_space=pl.ANY)
    return pl.pallas_call(
        fence_kernel,
        out_shape=jax.ShapeDtypeStruct(flag.shape, flag.dtype),
        in_specs=[vmem] + [hbm] * len(earlier) + [vmem] * len(resident),
        out_specs=vmem,
        compiler_params=pltpu.CompilerParams(vmem_limit_bytes=UP_VMEM if resident else SMALL_VMEM),
        cost_estimate=pl.CostEstimate(flops=20_000_000_000, bytes_accessed=0, transcendentals=0),
    )(flag, *earlier, *resident)


def halves_kernel(first_ref, second_ref, upper_ref, lower_ref):
    middle = upper_ref.shape[0]
    upper_ref[...] = first_ref[:middle]
    lower_ref[...] = second_ref[middle:]


def halves(first, second):
    rows, width = first.shape
    vmem = pl.BlockSpec(memory_space=pltpu.VMEM)
    shape = jax.ShapeDtypeStruct((rows // 2, width), first.dtype)
    return pl.pallas_call(
        halves_kernel,
        out_shape=[shape] * 2,
        in_specs=[vmem] * 2,
        out_specs=[vmem] * 2,
        compiler_params=pltpu.CompilerParams(vmem_limit_bytes=SMALL_VMEM),
    )(first, second)


def join_kernel(first_ref, second_ref, upper_ref, lower_ref, one_ref, other_ref):
    middle = upper_ref.shape[0]

    def plus(rows, more):
        return (rows.astype(jnp.float32) + more.astype(jnp.float32)).astype(jnp.bfloat16)

    one_ref[:middle] = plus(first_ref[:middle], upper_ref[...])
    one_ref[middle:] = first_ref[middle:]
    other_ref[:middle] = second_ref[:middle]
    other_ref[middle:] = plus(second_ref[middle:], lower_ref[...])


def join(first, second, upper, lower):
    vmem = pl.BlockSpec(memory_space=pltpu.VMEM)
    shape = jax.ShapeDtypeStruct(first.shape, first.dtype)
    return pl.pallas_call(
        join_kernel,
        out_shape=[shape] * 2,
        in_specs=[vmem] * 4,
        out_specs=[vmem] * 2,
        compiler_params=pltpu.CompilerParams(vmem_limit_bytes=SMALL_VMEM),
    )(first, second, upper, lower)


def fold(rows, size):
    bits = 2
    while bits < size:
        rows = [jnp.concatenate(rows, axis=0)]
        rows = [jnp.concatenate([rows[0], swap(rows[0], "tensor", bits)], axis=0)]
        bits *= 2
    return rows


def unfold(pieces, size):
    bits = size // 2
    while bits > 1:
        half = pieces[0].shape[0] // 2
        pieces = [add(pieces[0][:half], swap(pieces[0][half:], "tensor", bits))]
        bits //= 2
    if len(pieces) > 1:
        return pieces
    rows = pieces[0].shape[0]
    return jnp.split(pieces[0], [rows // 4, rows // 2, rows * 3 // 4, rows * 7 // 8])


def up_kernel(count, later, *refs):
    x_refs, refs = refs[:count], refs[count:]
    mine_ref, refs = refs[0], refs[1 + later :]
    gate_refs, up_refs, refs = refs[0:2], refs[2:4], refs[4:]
    hidden_ref, rows_in, weights, rows_sem, weights_sem = refs
    experts, width, units = gate_refs[0].shape
    row_copies, start = [], 0
    for n, x_ref in enumerate(x_refs):
        rows = x_ref.shape[0]
        row_copies.append(pltpu.make_async_copy(x_ref, rows_in.at[pl.ds(start, rows), :], rows_sem.at[n]))
        start += rows

    def parts_of(e):
        return UP_PARTS if e == 0 else 1

    def weight_copies(e, part):
        size = width // parts_of(e)
        span = pl.ds(part * size, size)
        return [
            pltpu.make_async_copy(
                ref.at[e % experts, span, :],
                weights.at[e % UP_SLOTS, span, pl.ds(side * units, units)],
                weights_sem.at[e % UP_SLOTS, part, side],
            )
            for side, ref in enumerate((gate_refs[e // experts], up_refs[e // experts]))
        ]

    def start_weights(e):
        if e < 2 * experts:
            for part in range(parts_of(e)):
                for copy in weight_copies(e, part):
                    copy.start()

    for copy in row_copies:
        copy.start()
    for e in range(UP_SLOTS - 1):
        start_weights(e)
    for copy in row_copies:
        copy.wait()
    for e in range(2 * experts):
        start_weights(e + UP_SLOTS - 1)
        for group in range(0, rows_in.shape[0], GROUP):
            rows = slice(group, group + GROUP)
            both = None
            for part in range(parts_of(e)):
                if group == 0:
                    for copy in weight_copies(e, part):
                        copy.wait()
                size = width // parts_of(e)
                span = slice(part * size, (part + 1) * size)
                term = jnp.dot(
                    rows_in[rows, span], weights[e % UP_SLOTS, span], preferred_element_type=jnp.float32
                )
                both = term if both is None else both + term
            gate_val, up_val = both[:, :units], both[:, units:]
            spare = rows_in[rows, width:].astype(jnp.float32)
            weight = jnp.sum(spare * mine_ref[e : e + 1, :], axis=1, keepdims=True)
            value = gate_val / (1.0 + jnp.exp(-gate_val)) * up_val * weight
            hidden_ref[rows, e * units : (e + 1) * units] = value.astype(jnp.bfloat16)


def up_block(pieces, mine, later, gates, ups):
    experts, width, units = gates[0].shape
    rows = sum(piece.shape[0] for piece in pieces)
    vmem = pl.BlockSpec(memory_space=pltpu.VMEM)
    hbm = pl.BlockSpec(memory_space=pl.ANY)
    return pl.pallas_call(
        functools.partial(up_kernel, len(pieces), len(later)),
        out_shape=jax.ShapeDtypeStruct((rows, 2 * experts * units), jnp.bfloat16),
        in_specs=[hbm] * len(pieces) + [vmem] + [hbm] * (len(later) + 4),
        out_specs=vmem,
        scratch_shapes=[
            pltpu.VMEM((rows, pieces[0].shape[1]), jnp.bfloat16),
            pltpu.VMEM((UP_SLOTS, width, 2 * units), jnp.bfloat16),
            pltpu.SemaphoreType.DMA((len(pieces),)),
            pltpu.SemaphoreType.DMA((UP_SLOTS, UP_PARTS, 2)),
        ],
        compiler_params=pltpu.CompilerParams(vmem_limit_bytes=UP_VMEM),
        cost_estimate=pl.CostEstimate(
            flops=8 * rows * experts * units * width,
            bytes_accessed=8 * experts * units * width + 2 * rows * width,
            transcendentals=2 * rows * experts * units,
        ),
    )(*pieces, mine, *later, *gates, *ups)


def down_kernel(count, later, first, hidden_ref, *refs):
    down_refs, refs = refs[later : later + 2], refs[later + 2 :]
    y_refs, (weights, weights_sem) = refs[:count], refs[count:]
    experts, units, width = down_refs[0].shape
    tiles = width // DOWN_TILE
    copies = [
        [
            pltpu.make_async_copy(
                down_refs[e // experts].at[e % experts, :, pl.ds(tile * DOWN_TILE, DOWN_TILE)],
                weights.at[tile, pl.ds(e * units, units), :],
                weights_sem.at[tile, e],
            )
            for e in range(2 * experts)
        ]
        for tile in range(tiles)
    ]
    for group in copies:
        for copy in group:
            copy.start()
    rows_in = slice(first, first + sum(y_ref.shape[0] for y_ref in y_refs))
    for tile in range(tiles):
        for copy in copies[tile]:
            copy.wait()
        cols = slice(tile * DOWN_TILE, (tile + 1) * DOWN_TILE)
        result = jnp.dot(
            hidden_ref[rows_in], weights[tile], preferred_element_type=jnp.float32
        ).astype(jnp.bfloat16)
        start = 0
        for y_ref in y_refs:
            rows = y_ref.shape[0]
            y_ref[:, cols] = result[start : start + rows]
            start += rows


def down_block(hidden, first, sizes, later, downs):
    experts, units, width = downs[0].shape
    rows = sum(sizes)
    vmem = pl.BlockSpec(memory_space=pltpu.VMEM)
    hbm = pl.BlockSpec(memory_space=pl.ANY)
    return pl.pallas_call(
        functools.partial(down_kernel, len(sizes), len(later), first),
        out_shape=[jax.ShapeDtypeStruct((size, width), jnp.bfloat16) for size in sizes],
        in_specs=[vmem] + [hbm] * (len(later) + 2),
        out_specs=[vmem] * len(sizes),
        scratch_shapes=[
            pltpu.VMEM((width // DOWN_TILE, 2 * experts * units, DOWN_TILE), jnp.bfloat16),
            pltpu.SemaphoreType.DMA((width // DOWN_TILE, 2 * experts)),
        ],
        compiler_params=pltpu.CompilerParams(vmem_limit_bytes=DOWN_VMEM),
        cost_estimate=pl.CostEstimate(
            flops=4 * rows * experts * units * width,
            bytes_accessed=4 * experts * units * width + 2 * rows * width,
            transcendentals=0,
        ),
    )(hidden, *later, *downs)


def on_device(
    query_rows,
    key_rows,
    value_rows,
    residual,
    out_proj,
    post_gain,
    router,
    routes,
    w_gate,
    w_up,
    w_down,
):
    gates_pair, ups_pair = [(w, swap(w, "tensor", 1)) for w in (w_gate, w_up)]
    local_tokens = query_rows.shape[1]
    local_heads = query_rows.shape[2] // HEAD_WIDTH
    group = QH // KVH
    kv_dev = max(1, local_heads // group)
    share = local_heads // kv_dev
    kv_first = lax.axis_index("tensor") * local_heads // group * HEAD_WIDTH
    my_ctx = lax.axis_index("ctx")
    pair = jnp.concatenate(
        [
            lax.dynamic_slice_in_dim(rows[0], kv_first, kv_dev * HEAD_WIDTH, axis=1)
            for rows in (key_rows, value_rows)
        ],
        axis=1,
    )
    contexts = lax.axis_size("ctx")
    pairs = jnp.concatenate([pair] + [swap(pair, "ctx", bits) for bits in range(1, contexts)], axis=0)
    within = jnp.arange(local_tokens)
    places = my_ctx * local_tokens + within
    key_places = jnp.concatenate([(my_ctx ^ bits) * local_tokens + within for bits in range(contexts)])
    qrot = rotate(query_rows[0], places).reshape(local_tokens, kv_dev, share, HEAD_WIDTH)
    krot = rotate(pairs[:, : kv_dev * HEAD_WIDTH], key_places)
    value_heads = pairs[:, kv_dev * HEAD_WIDTH :].reshape(-1, kv_dev, HEAD_WIDTH)
    attention_score = jnp.einsum(
        "qghd,kgd->ghqk", qrot, krot, preferred_element_type=jnp.float32
    ) / jnp.sqrt(jnp.float32(HEAD_WIDTH))
    causal = places[:, None] >= key_places[None, :]
    attention_score = jnp.where(causal, attention_score, jnp.float32(-1e30))
    peak = jnp.max(attention_score, axis=-1, keepdims=True)
    expon = jnp.where(causal, jnp.exp(attention_score - peak), jnp.float32(0.0))
    total = jnp.sum(expon, axis=-1)
    softmax_weights = expon.astype(jnp.bfloat16)
    summed_output = jnp.einsum(
        "ghqk,kgd->qghd", softmax_weights, value_heads, preferred_element_type=jnp.float32
    )
    attended = (
        (summed_output / jnp.transpose(total, (2, 0, 1))[..., None])
        .astype(jnp.bfloat16)
        .reshape(local_tokens, local_heads * HEAD_WIDTH)
    )
    projected = jnp.dot(attended, out_proj, preferred_element_type=jnp.float32)
    projected, other_gate, other_up = lax.optimization_barrier((projected, gates_pair[1], ups_pair[1]))
    gates_pair, ups_pair = (gates_pair[0], other_gate), (ups_pair[0], other_up)
    bits = lax.axis_size("tensor") // 2
    while bits:
        half = projected.shape[0] // 2
        high = (lax.axis_index("tensor") & bits) != 0
        keep = jnp.where(high, projected[half:], projected[:half])
        give = jnp.where(high, projected[:half], projected[half:])
        projected = keep + swap(give, "tensor", bits)
        bits //= 2
    mixed_wide = residual[0].astype(jnp.float32) + projected
    mixed = mixed_wide.astype(jnp.bfloat16)
    mixed, w_down = lax.optimization_barrier((mixed, w_down))
    downs_pair = w_down, swap(w_down, "tensor", 1)
    mixed_wide = mixed.astype(jnp.float32)
    scale = lax.rsqrt(jnp.mean(mixed_wide * mixed_wide, axis=-1, keepdims=True) + 1e-06)
    normed = (mixed_wide * scale * post_gain.astype(jnp.float32)).astype(jnp.bfloat16)
    logits = jnp.dot(normed, router, preferred_element_type=jnp.float32)
    picks = routes[0]
    tokens = picks.shape[0]
    experts_all = router.shape[1]
    chosen = jnp.any(picks[:, :, None] == jnp.arange(experts_all)[None, None, :], axis=1)
    peak_logit = jnp.max(jnp.where(chosen, logits, -jnp.inf), axis=1, keepdims=True)
    numer = jnp.where(chosen, jnp.exp(jnp.where(chosen, logits - peak_logit, 0.0)), 0.0)
    gates = numer / jnp.sum(numer, axis=1, keepdims=True)
    gates_high = gates.astype(jnp.bfloat16)
    gates_low = (gates - gates_high.astype(jnp.float32)).astype(jnp.bfloat16)
    lanes = -(-2 * experts_all // LANES) * LANES
    spare = jnp.zeros((tokens, lanes - 2 * experts_all), jnp.bfloat16)
    block = jnp.concatenate([normed, gates_high, gates_low, spare], axis=1)

    exp_dev = w_gate.shape[0]
    lane = jnp.arange(lanes)
    mine = []
    for core in (0, 1):
        group_id = lax.axis_index("ctx") * lax.axis_size("tensor") + (lax.axis_index("tensor") ^ core)
        for e in range(exp_dev):
            expert = group_id * exp_dev + e
            mine.append((lane == expert) | (lane == experts_all + expert))
    mine = jnp.stack(mine).astype(jnp.float32)

    cores = lax.axis_size("tensor")

    def out_near(rows):
        return [(rows, "ctx", 1), (rows, "ctx", 2)]

    def out_corner(near):
        upper, lower = halves(*near)
        return [(upper, "ctx", 2), (lower, "ctx", 1)]

    def back_corner(sums):
        return [(sums[3], "ctx", 2), (sums[4], "ctx", 1)]

    def back_near(sums, corner):
        first, second = join(sums[1], sums[2], *corner)
        return [(first, "ctx", 1), (second, "ctx", 2)]

    def up_of(blocks, later=()):
        pieces = [fold([own, *near, *corner], cores) for own, near, corner in blocks]
        sizes = [[piece.shape[0] for piece in group] for group in pieces]
        return up_block(sum(pieces, []), flag, later, gates_pair, ups_pair), sizes

    def down_of(hidden, n=0, later=()):
        rows, sizes = hidden
        return unfold(down_block(rows, n * sum(sizes[0]), sizes[n], later, downs_pair), cores)

    inward, outward = [(1, 2), (2, 1)], [(1, 0), (2, 3)]
    place = lax.axis_index("dp")
    inner = (place == 1) | (place == 2)

    flag = fence(mine, [block])
    (*near0, rows1, inner3), mine = exchange([*out_near(block), (block, "dp", 1), (block, "dp", inward)], mine)
    flag, other_down = lax.optimization_barrier((flag, downs_pair[1]))
    downs_pair = downs_pair[0], other_down
    (*got, inner2, outer2), flag = exchange(
        [*out_corner(near0), *out_near(rows1), (rows1, "dp", inward), (inner3, "dp", outward)], flag
    )
    corner0, near1 = got[:2], got[2:]
    rows2 = jnp.where(inner, inner2, outer2)
    flag = fence(flag, [*near0, rows1])
    (*got, outer3), flag = exchange([*out_corner(near1), *out_near(rows2), (inner2, "dp", outward)], flag)
    corner1, near2 = got[:2], got[2:]
    rows3 = jnp.where(inner, inner3, outer3)
    hidden01 = up_of([(block, near0, corner0), (rows1, near1, corner1)])
    got, _ = exchange([*out_corner(near2), *out_near(rows3)], hidden01[0])
    corner2, near3 = got[:2], got[2:]
    sums1 = down_of(hidden01, 1, [*near2, rows3])
    half1, _ = exchange(back_corner(sums1), flag)
    out3 = out_corner(near3)
    corner3, _ = exchange(out3, flag)
    hidden2 = up_of([(rows2, near2, corner2)], [sums1[0], out3[0][0]])
    *half1, _ = lax.optimization_barrier((*half1, hidden2[0]))
    back1 = back_near(sums1, half1)
    full1, _ = exchange(back1, flag)
    sums2 = down_of(hidden2, 0, [back1[0][0], corner3[0]])
    half2, _ = exchange(back_corner(sums2), flag)
    sums0 = down_of(hidden01, 0, [sums2[0]])
    back2 = back_near(sums2, half2)
    full2, _ = exchange(back2, flag)
    hidden3 = up_of([(rows3, near3, corner3)], [back2[0][0], *full1, sums0[0]])
    part1 = swap(add(sums1[0], *full1), "dp", 1)
    total2 = add(sums2[0], *full2)
    sums3 = down_of(hidden3, 0, [total2, part1])
    half3, _ = exchange(back_corner(sums3), flag)
    part2 = swap(total2, "dp", 2)
    back3 = back_near(sums3, half3)
    full3, _ = exchange(back3, flag)
    half0, part2 = exchange(back_corner(sums0), part2)
    total3 = add(sums3[0], *full3)
    (part3,), part2 = exchange([(total3, "dp", 3)], part2)
    full0, _ = exchange(back_near(sums0, half0), total3)
    moe_sum = sums0[0].astype(jnp.float32)
    for part in (*full0, part1, part2, part3):
        moe_sum = moe_sum + part.astype(jnp.float32)
    layer_out = (mixed_wide + moe_sum).astype(jnp.bfloat16)
    return layer_out[None]


def solution(mesh):
    in_specs = (
        P("dp", "ctx", "tensor"),
        P("dp", "ctx", None),
        P("dp", "ctx", None),
        P("dp", ("ctx", "tensor"), None),
        P("tensor", None),
        P(),
        P(),
        P("dp", ("ctx", "tensor"), None),
        P(("ctx", "tensor"), None, "dp"),
        P(("ctx", "tensor"), None, "dp"),
        P(("ctx", "tensor"), "dp", None),
    )
    out_specs = P("dp", ("ctx", "tensor"), None)
    return jax.shard_map(
        on_device, mesh=mesh, in_specs=in_specs, out_specs=out_specs, check_vma=False
    )
```

```python
import functools

import jax
import jax.numpy as jnp
from jax import lax
from jax.experimental import pallas as pl
from jax.experimental.pallas import tpu as pltpu
from jax.sharding import PartitionSpec as P

QH = 32
KVH = 2
HEAD_WIDTH = 128
LANES = 128
DOWN_TILE = 512
UP_VMEM = 36 * 1024 * 1024
UP_SLOTS = 3
GROUP = 256
UP_PARTS = 4
SMALL_VMEM = 4 * 1024 * 1024
DOWN_VMEM = 20 * 1024 * 1024


def rotate(rows, places):
    length = rows.shape[0]
    values = rows.astype(jnp.float32).reshape(length, -1, HEAD_WIDTH)
    half = HEAD_WIDTH // 2
    freqs = jnp.power(
        jnp.float32(1000000.0), -(jnp.arange(half).astype(jnp.float32) * 2.0 / HEAD_WIDTH)
    )
    angles = places.astype(jnp.float32)[:, None] * freqs[None, :]
    cosine = jnp.cos(angles)[:, None, :]
    sine = jnp.sin(angles)[:, None, :]
    first = values[..., :half]
    second = values[..., half:]
    turned = jnp.concatenate(
        [first * cosine - second * sine, second * cosine + first * sine], axis=-1
    )
    return turned.astype(jnp.bfloat16)


def swap(block, axis, bits):
    pairs = [(i, i ^ bits) for i in range(lax.axis_size(axis))] if isinstance(bits, int) else bits
    return lax.ppermute(block, axis, pairs)


def add(*terms):
    total = terms[0].astype(jnp.float32)
    for term in terms[1:]:
        total = total + term.astype(jnp.float32)
    return total.astype(jnp.bfloat16)


def exchange(moves, flag):
    *blocks, flag = lax.optimization_barrier((*[move[0] for move in moves], flag))
    return [swap(block, axis, bits) for block, (_, axis, bits) in zip(blocks, moves)], flag


def fence_kernel(flag_ref, *refs):
    refs[-1][...] = flag_ref[...]


def fence(flag, earlier, resident=()):
    vmem = pl.BlockSpec(memory_space=pltpu.VMEM)
    hbm = pl.BlockSpec(memory_space=pl.ANY)
    return pl.pallas_call(
        fence_kernel,
        out_shape=jax.ShapeDtypeStruct(flag.shape, flag.dtype),
        in_specs=[vmem] + [hbm] * len(earlier) + [vmem] * len(resident),
        out_specs=vmem,
        compiler_params=pltpu.CompilerParams(vmem_limit_bytes=UP_VMEM if resident else SMALL_VMEM),
        cost_estimate=pl.CostEstimate(flops=20_000_000_000, bytes_accessed=0, transcendentals=0),
    )(flag, *earlier, *resident)


def halves_kernel(first_ref, second_ref, upper_ref, lower_ref):
    middle = upper_ref.shape[0]
    upper_ref[...] = first_ref[:middle]
    lower_ref[...] = second_ref[middle:]


def halves(first, second):
    rows, width = first.shape
    vmem = pl.BlockSpec(memory_space=pltpu.VMEM)
    shape = jax.ShapeDtypeStruct((rows // 2, width), first.dtype)
    return pl.pallas_call(
        halves_kernel,
        out_shape=[shape] * 2,
        in_specs=[vmem] * 2,
        out_specs=[vmem] * 2,
        compiler_params=pltpu.CompilerParams(vmem_limit_bytes=SMALL_VMEM),
    )(first, second)


def join_kernel(first_ref, second_ref, upper_ref, lower_ref, one_ref, other_ref):
    middle = upper_ref.shape[0]

    def plus(rows, more):
        return (rows.astype(jnp.float32) + more.astype(jnp.float32)).astype(jnp.bfloat16)

    one_ref[:middle] = plus(first_ref[:middle], upper_ref[...])
    one_ref[middle:] = first_ref[middle:]
    other_ref[:middle] = second_ref[:middle]
    other_ref[middle:] = plus(second_ref[middle:], lower_ref[...])


def join(first, second, upper, lower):
    vmem = pl.BlockSpec(memory_space=pltpu.VMEM)
    shape = jax.ShapeDtypeStruct(first.shape, first.dtype)
    return pl.pallas_call(
        join_kernel,
        out_shape=[shape] * 2,
        in_specs=[vmem] * 4,
        out_specs=[vmem] * 2,
        compiler_params=pltpu.CompilerParams(vmem_limit_bytes=SMALL_VMEM),
    )(first, second, upper, lower)


def fold(rows, size):
    bits = 2
    while bits < size:
        rows = [jnp.concatenate(rows, axis=0)]
        rows = [jnp.concatenate([rows[0], swap(rows[0], "tensor", bits)], axis=0)]
        bits *= 2
    return rows


def unfold(pieces, size):
    bits = size // 2
    while bits > 1:
        half = pieces[0].shape[0] // 2
        pieces = [add(pieces[0][:half], swap(pieces[0][half:], "tensor", bits))]
        bits //= 2
    if len(pieces) > 1:
        return pieces
    rows = pieces[0].shape[0]
    return jnp.split(pieces[0], [rows // 4, rows // 2, rows * 3 // 4, rows * 7 // 8])


def up_kernel(count, later, *refs):
    x_refs, refs = refs[:count], refs[count:]
    mine_ref, refs = refs[0], refs[1 + later :]
    gate_refs, up_refs, refs = refs[0:2], refs[2:4], refs[4:]
    *hidden_refs, rows_in, weights, rows_sem, weights_sem = refs
    experts, width, units = gate_refs[0].shape
    row_copies, start = [], 0
    for n, x_ref in enumerate(x_refs):
        rows = x_ref.shape[0]
        row_copies.append(pltpu.make_async_copy(x_ref, rows_in.at[pl.ds(start, rows), :], rows_sem.at[n]))
        start += rows

    def parts_of(e):
        return UP_PARTS if e == 0 else 1

    def weight_copies(e, part):
        size = width // parts_of(e)
        span = pl.ds(part * size, size)
        return [
            pltpu.make_async_copy(
                ref.at[e % experts, span, :],
                weights.at[e % UP_SLOTS, span, pl.ds(side * units, units)],
                weights_sem.at[e % UP_SLOTS, part, side],
            )
            for side, ref in enumerate((gate_refs[e // experts], up_refs[e // experts]))
        ]

    def start_weights(e):
        if e < 2 * experts:
            for part in range(parts_of(e)):
                for copy in weight_copies(e, part):
                    copy.start()

    for copy in row_copies:
        copy.start()
    for e in range(UP_SLOTS - 1):
        start_weights(e)
    for copy in row_copies:
        copy.wait()
    for e in range(2 * experts):
        start_weights(e + UP_SLOTS - 1)
        for group in range(0, rows_in.shape[0], GROUP):
            rows = slice(group, group + GROUP)
            both = None
            for part in range(parts_of(e)):
                if group == 0:
                    for copy in weight_copies(e, part):
                        copy.wait()
                size = width // parts_of(e)
                span = slice(part * size, (part + 1) * size)
                term = jnp.dot(
                    rows_in[rows, span], weights[e % UP_SLOTS, span], preferred_element_type=jnp.float32
                )
                both = term if both is None else both + term
            gate_val, up_val = both[:, :units], both[:, units:]
            spare = rows_in[rows, width:].astype(jnp.float32)
            weight = jnp.sum(spare * mine_ref[e : e + 1, :], axis=1, keepdims=True)
            value = gate_val / (1.0 + jnp.exp(-gate_val)) * up_val * weight
            hidden_refs[group // GROUP][:, e * units : (e + 1) * units] = value.astype(jnp.bfloat16)


def up_block(pieces, mine, later, gates, ups):
    experts, width, units = gates[0].shape
    rows = sum(piece.shape[0] for piece in pieces)
    vmem = pl.BlockSpec(memory_space=pltpu.VMEM)
    hbm = pl.BlockSpec(memory_space=pl.ANY)
    return pl.pallas_call(
        functools.partial(up_kernel, len(pieces), len(later)),
        out_shape=[jax.ShapeDtypeStruct((GROUP, 2 * experts * units), jnp.bfloat16)] * (rows // GROUP),
        in_specs=[hbm] * len(pieces) + [vmem] + [hbm] * (len(later) + 4),
        out_specs=[vmem] * (rows // GROUP),
        scratch_shapes=[
            pltpu.VMEM((rows, pieces[0].shape[1]), jnp.bfloat16),
            pltpu.VMEM((UP_SLOTS, width, 2 * units), jnp.bfloat16),
            pltpu.SemaphoreType.DMA((len(pieces),)),
            pltpu.SemaphoreType.DMA((UP_SLOTS, UP_PARTS, 2)),
        ],
        compiler_params=pltpu.CompilerParams(vmem_limit_bytes=UP_VMEM),
        cost_estimate=pl.CostEstimate(
            flops=8 * rows * experts * units * width,
            bytes_accessed=8 * experts * units * width + 2 * rows * width,
            transcendentals=2 * rows * experts * units,
        ),
    )(*pieces, mine, *later, *gates, *ups)


def down_kernel(count, later, hidden_ref, *refs):
    down_refs, refs = refs[later : later + 2], refs[later + 2 :]
    y_refs, (weights, weights_sem) = refs[:count], refs[count:]
    experts, units, width = down_refs[0].shape
    tiles = width // DOWN_TILE
    copies = [
        [
            pltpu.make_async_copy(
                down_refs[e // experts].at[e % experts, :, pl.ds(tile * DOWN_TILE, DOWN_TILE)],
                weights.at[tile, pl.ds(e * units, units), :],
                weights_sem.at[tile, e],
            )
            for e in range(2 * experts)
        ]
        for tile in range(tiles)
    ]
    for group in copies:
        for copy in group:
            copy.start()
    for tile in range(tiles):
        for copy in copies[tile]:
            copy.wait()
        cols = slice(tile * DOWN_TILE, (tile + 1) * DOWN_TILE)
        result = jnp.dot(
            hidden_ref[...], weights[tile], preferred_element_type=jnp.float32
        ).astype(jnp.bfloat16)
        start = 0
        for y_ref in y_refs:
            rows = y_ref.shape[0]
            y_ref[:, cols] = result[start : start + rows]
            start += rows


def down_block(hidden, sizes, later, downs):
    experts, units, width = downs[0].shape
    rows = hidden.shape[0]
    vmem = pl.BlockSpec(memory_space=pltpu.VMEM)
    hbm = pl.BlockSpec(memory_space=pl.ANY)
    return pl.pallas_call(
        functools.partial(down_kernel, len(sizes), len(later)),
        out_shape=[jax.ShapeDtypeStruct((size, width), jnp.bfloat16) for size in sizes],
        in_specs=[vmem] + [hbm] * (len(later) + 2),
        out_specs=[vmem] * len(sizes),
        scratch_shapes=[
            pltpu.VMEM((width // DOWN_TILE, 2 * experts * units, DOWN_TILE), jnp.bfloat16),
            pltpu.SemaphoreType.DMA((width // DOWN_TILE, 2 * experts)),
        ],
        compiler_params=pltpu.CompilerParams(vmem_limit_bytes=DOWN_VMEM),
        cost_estimate=pl.CostEstimate(
            flops=4 * rows * experts * units * width,
            bytes_accessed=4 * experts * units * width + 2 * rows * width,
            transcendentals=0,
        ),
    )(hidden, *later, *downs)


def on_device(
    query_rows,
    key_rows,
    value_rows,
    residual,
    out_proj,
    post_gain,
    router,
    routes,
    w_gate,
    w_up,
    w_down,
):
    gates_pair, ups_pair = [(w, swap(w, "tensor", 1)) for w in (w_gate, w_up)]
    local_tokens = query_rows.shape[1]
    local_heads = query_rows.shape[2] // HEAD_WIDTH
    group = QH // KVH
    kv_dev = max(1, local_heads // group)
    share = local_heads // kv_dev
    kv_first = lax.axis_index("tensor") * local_heads // group * HEAD_WIDTH
    my_ctx = lax.axis_index("ctx")
    pair = jnp.concatenate(
        [
            lax.dynamic_slice_in_dim(rows[0], kv_first, kv_dev * HEAD_WIDTH, axis=1)
            for rows in (key_rows, value_rows)
        ],
        axis=1,
    )
    contexts = lax.axis_size("ctx")
    pairs = jnp.concatenate([pair] + [swap(pair, "ctx", bits) for bits in range(1, contexts)], axis=0)
    within = jnp.arange(local_tokens)
    places = my_ctx * local_tokens + within
    key_places = jnp.concatenate([(my_ctx ^ bits) * local_tokens + within for bits in range(contexts)])
    qrot = rotate(query_rows[0], places).reshape(local_tokens, kv_dev, share, HEAD_WIDTH)
    krot = rotate(pairs[:, : kv_dev * HEAD_WIDTH], key_places)
    value_heads = pairs[:, kv_dev * HEAD_WIDTH :].reshape(-1, kv_dev, HEAD_WIDTH)
    attention_score = jnp.einsum(
        "qghd,kgd->ghqk", qrot, krot, preferred_element_type=jnp.float32
    ) / jnp.sqrt(jnp.float32(HEAD_WIDTH))
    causal = places[:, None] >= key_places[None, :]
    attention_score = jnp.where(causal, attention_score, jnp.float32(-1e30))
    peak = jnp.max(attention_score, axis=-1, keepdims=True)
    expon = jnp.where(causal, jnp.exp(attention_score - peak), jnp.float32(0.0))
    total = jnp.sum(expon, axis=-1)
    softmax_weights = expon.astype(jnp.bfloat16)
    summed_output = jnp.einsum(
        "ghqk,kgd->qghd", softmax_weights, value_heads, preferred_element_type=jnp.float32
    )
    attended = (
        (summed_output / jnp.transpose(total, (2, 0, 1))[..., None])
        .astype(jnp.bfloat16)
        .reshape(local_tokens, local_heads * HEAD_WIDTH)
    )
    projected = jnp.dot(attended, out_proj, preferred_element_type=jnp.float32)
    projected, other_gate, other_up = lax.optimization_barrier((projected, gates_pair[1], ups_pair[1]))
    gates_pair, ups_pair = (gates_pair[0], other_gate), (ups_pair[0], other_up)
    bits = lax.axis_size("tensor") // 2
    while bits:
        half = projected.shape[0] // 2
        high = (lax.axis_index("tensor") & bits) != 0
        keep = jnp.where(high, projected[half:], projected[:half])
        give = jnp.where(high, projected[:half], projected[half:])
        projected = keep + swap(give, "tensor", bits)
        bits //= 2
    mixed_wide = residual[0].astype(jnp.float32) + projected
    mixed = mixed_wide.astype(jnp.bfloat16)
    mixed, w_down = lax.optimization_barrier((mixed, w_down))
    downs_pair = w_down, swap(w_down, "tensor", 1)
    mixed_wide = mixed.astype(jnp.float32)
    scale = lax.rsqrt(jnp.mean(mixed_wide * mixed_wide, axis=-1, keepdims=True) + 1e-06)
    normed = (mixed_wide * scale * post_gain.astype(jnp.float32)).astype(jnp.bfloat16)
    logits = jnp.dot(normed, router, preferred_element_type=jnp.float32)
    picks = routes[0]
    tokens = picks.shape[0]
    experts_all = router.shape[1]
    chosen = jnp.any(picks[:, :, None] == jnp.arange(experts_all)[None, None, :], axis=1)
    peak_logit = jnp.max(jnp.where(chosen, logits, -jnp.inf), axis=1, keepdims=True)
    numer = jnp.where(chosen, jnp.exp(jnp.where(chosen, logits - peak_logit, 0.0)), 0.0)
    gates = numer / jnp.sum(numer, axis=1, keepdims=True)
    gates_high = gates.astype(jnp.bfloat16)
    gates_low = (gates - gates_high.astype(jnp.float32)).astype(jnp.bfloat16)
    lanes = -(-2 * experts_all // LANES) * LANES
    spare = jnp.zeros((tokens, lanes - 2 * experts_all), jnp.bfloat16)
    block = jnp.concatenate([normed, gates_high, gates_low, spare], axis=1)

    exp_dev = w_gate.shape[0]
    lane = jnp.arange(lanes)
    mine = []
    for core in (0, 1):
        group_id = lax.axis_index("ctx") * lax.axis_size("tensor") + (lax.axis_index("tensor") ^ core)
        for e in range(exp_dev):
            expert = group_id * exp_dev + e
            mine.append((lane == expert) | (lane == experts_all + expert))
    mine = jnp.stack(mine).astype(jnp.float32)

    cores = lax.axis_size("tensor")

    def out_near(rows):
        return [(rows, "ctx", 1), (rows, "ctx", 2)]

    def out_corner(near):
        upper, lower = halves(*near)
        return [(upper, "ctx", 2), (lower, "ctx", 1)]

    def back_corner(sums):
        return [(sums[3], "ctx", 2), (sums[4], "ctx", 1)]

    def back_near(sums, corner):
        first, second = join(sums[1], sums[2], *corner)
        return [(first, "ctx", 1), (second, "ctx", 2)]

    def up_of(blocks, later=()):
        pieces = [fold([own, *near, *corner], cores) for own, near, corner in blocks]
        sizes = [[piece.shape[0] for piece in group] for group in pieces]
        return up_block(sum(pieces, []), flag, later, gates_pair, ups_pair), sizes

    def down_of(hidden, n=0, later=()):
        rows, sizes = hidden
        return unfold(down_block(rows[n], sizes[n], later, downs_pair), cores)

    inward, outward = [(1, 2), (2, 1)], [(1, 0), (2, 3)]
    place = lax.axis_index("dp")
    inner = (place == 1) | (place == 2)

    flag = fence(mine, [block])
    (*near0, rows1, inner3), mine = exchange([*out_near(block), (block, "dp", 1), (block, "dp", inward)], mine)
    flag, other_down = lax.optimization_barrier((flag, downs_pair[1]))
    downs_pair = downs_pair[0], other_down
    (*got, inner2, outer2), flag = exchange(
        [*out_corner(near0), *out_near(rows1), (rows1, "dp", inward), (inner3, "dp", outward)], flag
    )
    corner0, near1 = got[:2], got[2:]
    rows2 = jnp.where(inner, inner2, outer2)
    flag = fence(flag, [*near0, rows1])
    (*got, outer3), flag = exchange([*out_corner(near1), *out_near(rows2), (inner2, "dp", outward)], flag)
    corner1, near2 = got[:2], got[2:]
    rows3 = jnp.where(inner, inner3, outer3)
    hidden01 = up_of([(block, near0, corner0), (rows1, near1, corner1)])
    got, _ = exchange([*out_corner(near2), *out_near(rows3)], hidden01[0][0])
    corner2, near3 = got[:2], got[2:]
    sums1 = down_of(hidden01, 1, [*near2, rows3])
    half1, _ = exchange(back_corner(sums1), flag)
    out3 = out_corner(near3)
    corner3, _ = exchange(out3, flag)
    hidden2 = up_of([(rows2, near2, corner2)], [sums1[0], out3[0][0]])
    *half1, _ = lax.optimization_barrier((*half1, hidden2[0][0]))
    back1 = back_near(sums1, half1)
    full1, _ = exchange(back1, flag)
    sums2 = down_of(hidden2, 0, [back1[0][0], corner3[0]])
    half2, _ = exchange(back_corner(sums2), flag)
    sums0 = down_of(hidden01, 0, [sums2[0]])
    back2 = back_near(sums2, half2)
    full2, _ = exchange(back2, flag)
    hidden3 = up_of([(rows3, near3, corner3)], [back2[0][0], *full1, sums0[0]])
    part1 = swap(add(sums1[0], *full1), "dp", 1)
    total2 = add(sums2[0], *full2)
    sums3 = down_of(hidden3, 0, [total2, part1])
    half3, _ = exchange(back_corner(sums3), flag)
    part2 = swap(total2, "dp", 2)
    back3 = back_near(sums3, half3)
    full3, _ = exchange(back3, flag)
    half0, part2 = exchange(back_corner(sums0), part2)
    total3 = add(sums3[0], *full3)
    (part3,), part2 = exchange([(total3, "dp", 3)], part2)
    *half0, flag = lax.optimization_barrier((*half0, fence(flag, [total3])))
    full0, _ = exchange(back_near(sums0, half0), flag)
    moe_sum = sums0[0].astype(jnp.float32)
    for part in (*full0, part1, part2, part3):
        moe_sum = moe_sum + part.astype(jnp.float32)
    layer_out = (mixed_wide + moe_sum).astype(jnp.bfloat16)
    return layer_out[None]


def solution(mesh):
    in_specs = (
        P("dp", "ctx", "tensor"),
        P("dp", "ctx", None),
        P("dp", "ctx", None),
        P("dp", ("ctx", "tensor"), None),
        P("tensor", None),
        P(),
        P(),
        P("dp", ("ctx", "tensor"), None),
        P(("ctx", "tensor"), None, "dp"),
        P(("ctx", "tensor"), None, "dp"),
        P(("ctx", "tensor"), "dp", None),
    )
    out_specs = P("dp", ("ctx", "tensor"), None)
    return jax.shard_map(
        on_device, mesh=mesh, in_specs=in_specs, out_specs=out_specs, check_vma=False
    )
```

```python
import functools

import jax
import jax.numpy as jnp
from jax import lax
from jax.experimental import pallas as pl
from jax.experimental.pallas import tpu as pltpu
from jax.sharding import PartitionSpec as P

QH = 32
KVH = 2
HEAD_WIDTH = 128
LANES = 128
DOWN_TILE = 512
UP_VMEM = 36 * 1024 * 1024
UP_SLOTS = 3
GROUP = 256
UP_PARTS = 4
SMALL_VMEM = 4 * 1024 * 1024
DOWN_VMEM = 20 * 1024 * 1024


def rotate(rows, places):
    length = rows.shape[0]
    values = rows.astype(jnp.float32).reshape(length, -1, HEAD_WIDTH)
    half = HEAD_WIDTH // 2
    freqs = jnp.power(
        jnp.float32(1000000.0), -(jnp.arange(half).astype(jnp.float32) * 2.0 / HEAD_WIDTH)
    )
    angles = places.astype(jnp.float32)[:, None] * freqs[None, :]
    cosine = jnp.cos(angles)[:, None, :]
    sine = jnp.sin(angles)[:, None, :]
    first = values[..., :half]
    second = values[..., half:]
    turned = jnp.concatenate(
        [first * cosine - second * sine, second * cosine + first * sine], axis=-1
    )
    return turned.astype(jnp.bfloat16)


def swap(block, axis, bits):
    pairs = [(i, i ^ bits) for i in range(lax.axis_size(axis))] if isinstance(bits, int) else bits
    return lax.ppermute(block, axis, pairs)


def add(*terms):
    total = terms[0].astype(jnp.float32)
    for term in terms[1:]:
        total = total + term.astype(jnp.float32)
    return total.astype(jnp.bfloat16)


def exchange(moves, flag):
    *blocks, flag = lax.optimization_barrier((*[move[0] for move in moves], flag))
    return [swap(block, axis, bits) for block, (_, axis, bits) in zip(blocks, moves)], flag


def fence_kernel(flag_ref, *refs):
    refs[-1][...] = flag_ref[...]


def fence(flag, earlier, resident=()):
    vmem = pl.BlockSpec(memory_space=pltpu.VMEM)
    hbm = pl.BlockSpec(memory_space=pl.ANY)
    return pl.pallas_call(
        fence_kernel,
        out_shape=jax.ShapeDtypeStruct(flag.shape, flag.dtype),
        in_specs=[vmem] + [hbm] * len(earlier) + [vmem] * len(resident),
        out_specs=vmem,
        compiler_params=pltpu.CompilerParams(vmem_limit_bytes=UP_VMEM if resident else SMALL_VMEM),
        cost_estimate=pl.CostEstimate(flops=20_000_000_000, bytes_accessed=0, transcendentals=0),
    )(flag, *earlier, *resident)


def halves_kernel(first_ref, second_ref, upper_ref, lower_ref):
    middle = upper_ref.shape[0]
    upper_ref[...] = first_ref[:middle]
    lower_ref[...] = second_ref[middle:]


def halves(first, second):
    rows, width = first.shape
    vmem = pl.BlockSpec(memory_space=pltpu.VMEM)
    shape = jax.ShapeDtypeStruct((rows // 2, width), first.dtype)
    return pl.pallas_call(
        halves_kernel,
        out_shape=[shape] * 2,
        in_specs=[vmem] * 2,
        out_specs=[vmem] * 2,
        compiler_params=pltpu.CompilerParams(vmem_limit_bytes=SMALL_VMEM),
    )(first, second)


def join_kernel(first_ref, second_ref, upper_ref, lower_ref, one_ref, other_ref):
    middle = upper_ref.shape[0]

    def plus(rows, more):
        return (rows.astype(jnp.float32) + more.astype(jnp.float32)).astype(jnp.bfloat16)

    one_ref[:middle] = plus(first_ref[:middle], upper_ref[...])
    one_ref[middle:] = first_ref[middle:]
    other_ref[:middle] = second_ref[:middle]
    other_ref[middle:] = plus(second_ref[middle:], lower_ref[...])


def join(first, second, upper, lower):
    vmem = pl.BlockSpec(memory_space=pltpu.VMEM)
    shape = jax.ShapeDtypeStruct(first.shape, first.dtype)
    return pl.pallas_call(
        join_kernel,
        out_shape=[shape] * 2,
        in_specs=[vmem] * 4,
        out_specs=[vmem] * 2,
        compiler_params=pltpu.CompilerParams(vmem_limit_bytes=SMALL_VMEM),
    )(first, second, upper, lower)


def fold(rows, size):
    bits = 2
    while bits < size:
        rows = [jnp.concatenate(rows, axis=0)]
        rows = [jnp.concatenate([rows[0], swap(rows[0], "tensor", bits)], axis=0)]
        bits *= 2
    return rows


def unfold(pieces, size):
    bits = size // 2
    while bits > 1:
        half = pieces[0].shape[0] // 2
        pieces = [add(pieces[0][:half], swap(pieces[0][half:], "tensor", bits))]
        bits //= 2
    if len(pieces) > 1:
        return pieces
    rows = pieces[0].shape[0]
    return jnp.split(pieces[0], [rows // 4, rows // 2, rows * 3 // 4, rows * 7 // 8])


def up_kernel(count, later, *refs):
    x_refs, refs = refs[:count], refs[count:]
    mine_ref, refs = refs[0], refs[1 + later :]
    gate_refs, up_refs, refs = refs[0:2], refs[2:4], refs[4:]
    *hidden_refs, rows_in, weights, rows_sem, weights_sem = refs
    experts, width, units = gate_refs[0].shape
    row_copies, start = [], 0
    for n, x_ref in enumerate(x_refs):
        rows = x_ref.shape[0]
        row_copies.append(pltpu.make_async_copy(x_ref, rows_in.at[pl.ds(start, rows), :], rows_sem.at[n]))
        start += rows

    def parts_of(e):
        return UP_PARTS if e == 0 else 1

    def weight_copies(e, part):
        size = width // parts_of(e)
        span = pl.ds(part * size, size)
        return [
            pltpu.make_async_copy(
                ref.at[e % experts, span, :],
                weights.at[e % UP_SLOTS, span, pl.ds(side * units, units)],
                weights_sem.at[e % UP_SLOTS, part, side],
            )
            for side, ref in enumerate((gate_refs[e // experts], up_refs[e // experts]))
        ]

    def start_weights(e):
        if e < 2 * experts:
            for part in range(parts_of(e)):
                for copy in weight_copies(e, part):
                    copy.start()

    for copy in row_copies:
        copy.start()
    for e in range(UP_SLOTS - 1):
        start_weights(e)
    for copy in row_copies:
        copy.wait()
    for e in range(2 * experts):
        start_weights(e + UP_SLOTS - 1)
        for group in range(0, rows_in.shape[0], GROUP):
            rows = slice(group, group + GROUP)
            both = None
            for part in range(parts_of(e)):
                if group == 0:
                    for copy in weight_copies(e, part):
                        copy.wait()
                size = width // parts_of(e)
                span = slice(part * size, (part + 1) * size)
                term = jnp.dot(
                    rows_in[rows, span], weights[e % UP_SLOTS, span], preferred_element_type=jnp.float32
                )
                both = term if both is None else both + term
            gate_val, up_val = both[:, :units], both[:, units:]
            spare = rows_in[rows, width:].astype(jnp.float32)
            weight = jnp.sum(spare * mine_ref[e : e + 1, :], axis=1, keepdims=True)
            value = gate_val / (1.0 + jnp.exp(-gate_val)) * up_val * weight
            hidden_refs[group // GROUP][:, e * units : (e + 1) * units] = value.astype(jnp.bfloat16)


def up_block(pieces, mine, later, gates, ups):
    experts, width, units = gates[0].shape
    rows = sum(piece.shape[0] for piece in pieces)
    vmem = pl.BlockSpec(memory_space=pltpu.VMEM)
    hbm = pl.BlockSpec(memory_space=pl.ANY)
    return pl.pallas_call(
        functools.partial(up_kernel, len(pieces), len(later)),
        out_shape=[jax.ShapeDtypeStruct((GROUP, 2 * experts * units), jnp.bfloat16)] * (rows // GROUP),
        in_specs=[hbm] * len(pieces) + [vmem] + [hbm] * (len(later) + 4),
        out_specs=[vmem] * (rows // GROUP),
        scratch_shapes=[
            pltpu.VMEM((rows, pieces[0].shape[1]), jnp.bfloat16),
            pltpu.VMEM((UP_SLOTS, width, 2 * units), jnp.bfloat16),
            pltpu.SemaphoreType.DMA((len(pieces),)),
            pltpu.SemaphoreType.DMA((UP_SLOTS, UP_PARTS, 2)),
        ],
        compiler_params=pltpu.CompilerParams(vmem_limit_bytes=UP_VMEM),
        cost_estimate=pl.CostEstimate(
            flops=8 * rows * experts * units * width,
            bytes_accessed=8 * experts * units * width + 2 * rows * width,
            transcendentals=2 * rows * experts * units,
        ),
    )(*pieces, mine, *later, *gates, *ups)


def down_kernel(count, later, hidden_ref, *refs):
    down_refs, refs = refs[later : later + 2], refs[later + 2 :]
    y_refs, (weights, weights_sem) = refs[:count], refs[count:]
    experts, units, width = down_refs[0].shape
    tiles = width // DOWN_TILE
    copies = [
        [
            pltpu.make_async_copy(
                down_refs[e // experts].at[e % experts, :, pl.ds(tile * DOWN_TILE, DOWN_TILE)],
                weights.at[tile, pl.ds(e * units, units), :],
                weights_sem.at[tile, e],
            )
            for e in range(2 * experts)
        ]
        for tile in range(tiles)
    ]
    for group in copies:
        for copy in group:
            copy.start()
    for tile in range(tiles):
        for copy in copies[tile]:
            copy.wait()
        cols = slice(tile * DOWN_TILE, (tile + 1) * DOWN_TILE)
        result = jnp.dot(
            hidden_ref[...], weights[tile], preferred_element_type=jnp.float32
        ).astype(jnp.bfloat16)
        start = 0
        for y_ref in y_refs:
            rows = y_ref.shape[0]
            y_ref[:, cols] = result[start : start + rows]
            start += rows


def down_block(hidden, sizes, later, downs):
    experts, units, width = downs[0].shape
    rows = hidden.shape[0]
    vmem = pl.BlockSpec(memory_space=pltpu.VMEM)
    hbm = pl.BlockSpec(memory_space=pl.ANY)
    return pl.pallas_call(
        functools.partial(down_kernel, len(sizes), len(later)),
        out_shape=[jax.ShapeDtypeStruct((size, width), jnp.bfloat16) for size in sizes],
        in_specs=[vmem] + [hbm] * (len(later) + 2),
        out_specs=[vmem] * len(sizes),
        scratch_shapes=[
            pltpu.VMEM((width // DOWN_TILE, 2 * experts * units, DOWN_TILE), jnp.bfloat16),
            pltpu.SemaphoreType.DMA((width // DOWN_TILE, 2 * experts)),
        ],
        compiler_params=pltpu.CompilerParams(vmem_limit_bytes=DOWN_VMEM),
        cost_estimate=pl.CostEstimate(
            flops=4 * rows * experts * units * width,
            bytes_accessed=4 * experts * units * width + 2 * rows * width,
            transcendentals=0,
        ),
    )(hidden, *later, *downs)


def on_device(
    query_rows,
    key_rows,
    value_rows,
    residual,
    out_proj,
    post_gain,
    router,
    routes,
    w_gate,
    w_up,
    w_down,
):
    gates_pair, ups_pair = [(w, swap(w, "tensor", 1)) for w in (w_gate, w_up)]
    local_tokens = query_rows.shape[1]
    local_heads = query_rows.shape[2] // HEAD_WIDTH
    group = QH // KVH
    kv_dev = max(1, local_heads // group)
    share = local_heads // kv_dev
    kv_first = lax.axis_index("tensor") * local_heads // group * HEAD_WIDTH
    my_ctx = lax.axis_index("ctx")
    pair = jnp.concatenate(
        [
            lax.dynamic_slice_in_dim(rows[0], kv_first, kv_dev * HEAD_WIDTH, axis=1)
            for rows in (key_rows, value_rows)
        ],
        axis=1,
    )
    contexts = lax.axis_size("ctx")
    pairs = jnp.concatenate([pair] + [swap(pair, "ctx", bits) for bits in range(1, contexts)], axis=0)
    within = jnp.arange(local_tokens)
    places = my_ctx * local_tokens + within
    key_places = jnp.concatenate([(my_ctx ^ bits) * local_tokens + within for bits in range(contexts)])
    qrot = rotate(query_rows[0], places).reshape(local_tokens, kv_dev, share, HEAD_WIDTH)
    krot = rotate(pairs[:, : kv_dev * HEAD_WIDTH], key_places)
    value_heads = pairs[:, kv_dev * HEAD_WIDTH :].reshape(-1, kv_dev, HEAD_WIDTH)
    attention_score = jnp.einsum(
        "qghd,kgd->ghqk", qrot, krot, preferred_element_type=jnp.float32
    ) / jnp.sqrt(jnp.float32(HEAD_WIDTH))
    causal = places[:, None] >= key_places[None, :]
    attention_score = jnp.where(causal, attention_score, jnp.float32(-1e30))
    peak = jnp.max(attention_score, axis=-1, keepdims=True)
    expon = jnp.where(causal, jnp.exp(attention_score - peak), jnp.float32(0.0))
    total = jnp.sum(expon, axis=-1)
    softmax_weights = expon.astype(jnp.bfloat16)
    summed_output = jnp.einsum(
        "ghqk,kgd->qghd", softmax_weights, value_heads, preferred_element_type=jnp.float32
    )
    attended = (
        (summed_output / jnp.transpose(total, (2, 0, 1))[..., None])
        .astype(jnp.bfloat16)
        .reshape(local_tokens, local_heads * HEAD_WIDTH)
    )
    projected = jnp.dot(attended, out_proj, preferred_element_type=jnp.float32)
    projected, other_gate, other_up = lax.optimization_barrier((projected, gates_pair[1], ups_pair[1]))
    gates_pair, ups_pair = (gates_pair[0], other_gate), (ups_pair[0], other_up)
    bits = lax.axis_size("tensor") // 2
    while bits:
        half = projected.shape[0] // 2
        high = (lax.axis_index("tensor") & bits) != 0
        keep = jnp.where(high, projected[half:], projected[:half])
        give = jnp.where(high, projected[:half], projected[half:])
        projected = keep + swap(give, "tensor", bits)
        bits //= 2
    mixed_wide = residual[0].astype(jnp.float32) + projected
    mixed = mixed_wide.astype(jnp.bfloat16)
    mixed, w_down = lax.optimization_barrier((mixed, w_down))
    downs_pair = w_down, swap(w_down, "tensor", 1)
    mixed_wide = mixed.astype(jnp.float32)
    scale = lax.rsqrt(jnp.mean(mixed_wide * mixed_wide, axis=-1, keepdims=True) + 1e-06)
    normed = (mixed_wide * scale * post_gain.astype(jnp.float32)).astype(jnp.bfloat16)
    logits = jnp.dot(normed, router, preferred_element_type=jnp.float32)
    picks = routes[0]
    tokens = picks.shape[0]
    experts_all = router.shape[1]
    chosen = jnp.any(picks[:, :, None] == jnp.arange(experts_all)[None, None, :], axis=1)
    peak_logit = jnp.max(jnp.where(chosen, logits, -jnp.inf), axis=1, keepdims=True)
    numer = jnp.where(chosen, jnp.exp(jnp.where(chosen, logits - peak_logit, 0.0)), 0.0)
    gates = numer / jnp.sum(numer, axis=1, keepdims=True)
    gates_high = gates.astype(jnp.bfloat16)
    gates_low = (gates - gates_high.astype(jnp.float32)).astype(jnp.bfloat16)
    lanes = -(-2 * experts_all // LANES) * LANES
    spare = jnp.zeros((tokens, lanes - 2 * experts_all), jnp.bfloat16)
    block = jnp.concatenate([normed, gates_high, gates_low, spare], axis=1)

    exp_dev = w_gate.shape[0]
    lane = jnp.arange(lanes)
    mine = []
    for core in (0, 1):
        group_id = lax.axis_index("ctx") * lax.axis_size("tensor") + (lax.axis_index("tensor") ^ core)
        for e in range(exp_dev):
            expert = group_id * exp_dev + e
            mine.append((lane == expert) | (lane == experts_all + expert))
    mine = jnp.stack(mine).astype(jnp.float32)

    cores = lax.axis_size("tensor")

    def out_near(rows):
        return [(rows, "ctx", 1), (rows, "ctx", 2)]

    def out_corner(near):
        upper, lower = halves(*near)
        return [(upper, "ctx", 2), (lower, "ctx", 1)]

    def back_corner(sums):
        return [(sums[3], "ctx", 2), (sums[4], "ctx", 1)]

    def back_near(sums, corner):
        first, second = join(sums[1], sums[2], *corner)
        return [(first, "ctx", 1), (second, "ctx", 2)]

    def up_of(blocks, later=()):
        pieces = [fold([own, *near, *corner], cores) for own, near, corner in blocks]
        sizes = [[piece.shape[0] for piece in group] for group in pieces]
        return up_block(sum(pieces, []), flag, later, gates_pair, ups_pair), sizes

    def down_of(hidden, n=0, later=()):
        rows, sizes = hidden
        return unfold(down_block(rows[n], sizes[n], later, downs_pair), cores)

    inward, outward = [(1, 2), (2, 1)], [(1, 0), (2, 3)]
    place = lax.axis_index("dp")
    inner = (place == 1) | (place == 2)

    flag = fence(mine, [block])
    (*near0, rows1, inner3), mine = exchange([*out_near(block), (block, "dp", 1), (block, "dp", inward)], mine)
    flag, other_down = lax.optimization_barrier((flag, downs_pair[1]))
    downs_pair = downs_pair[0], other_down
    (*got, inner2, outer2), flag = exchange(
        [*out_corner(near0), *out_near(rows1), (rows1, "dp", inward), (inner3, "dp", outward)], flag
    )
    corner0, near1 = got[:2], got[2:]
    rows2 = jnp.where(inner, inner2, outer2)
    flag = fence(flag, [*near0, rows1])
    (*got, outer3), flag = exchange([*out_corner(near1), *out_near(rows2), (inner2, "dp", outward)], flag)
    corner1, near2 = got[:2], got[2:]
    rows3 = jnp.where(inner, inner3, outer3)
    hidden0 = up_of([(block, near0, corner0)])
    got, _ = exchange([*out_corner(near2), *out_near(rows3)], hidden0[0][0])
    corner2, near3 = got[:2], got[2:]
    hidden1 = up_of([(rows1, near1, corner1)], [hidden0[0][0], *near2, rows3])
    sums1 = down_of(hidden1, 0, near3)
    half1, _ = exchange(back_corner(sums1), flag)
    out3 = out_corner(near3)
    corner3, _ = exchange(out3, flag)
    hidden2 = up_of([(rows2, near2, corner2)], [sums1[0], out3[0][0]])
    *half1, _ = lax.optimization_barrier((*half1, hidden2[0][0]))
    back1 = back_near(sums1, half1)
    full1, _ = exchange(back1, flag)
    sums2 = down_of(hidden2, 0, [back1[0][0], corner3[0]])
    half2, _ = exchange(back_corner(sums2), flag)
    sums0 = down_of(hidden0, 0, [sums2[0]])
    back2 = back_near(sums2, half2)
    full2, _ = exchange(back2, flag)
    hidden3 = up_of([(rows3, near3, corner3)], [back2[0][0], *full1, sums0[0]])
    part1 = swap(add(sums1[0], *full1), "dp", 1)
    total2 = add(sums2[0], *full2)
    sums3 = down_of(hidden3, 0, [total2, part1])
    half3, _ = exchange(back_corner(sums3), flag)
    part2 = swap(total2, "dp", 2)
    back3 = back_near(sums3, half3)
    full3, _ = exchange(back3, flag)
    half0, part2 = exchange(back_corner(sums0), part2)
    total3 = add(sums3[0], *full3)
    (part3,), part2 = exchange([(total3, "dp", 3)], part2)
    *half0, _ = lax.optimization_barrier((*half0, total3))
    full0, _ = exchange(back_near(sums0, half0), total3)
    moe_sum = sums0[0].astype(jnp.float32)
    for part in (*full0, part1, part2, part3):
        moe_sum = moe_sum + part.astype(jnp.float32)
    layer_out = (mixed_wide + moe_sum).astype(jnp.bfloat16)
    return layer_out[None]


def solution(mesh):
    in_specs = (
        P("dp", "ctx", "tensor"),
        P("dp", "ctx", None),
        P("dp", "ctx", None),
        P("dp", ("ctx", "tensor"), None),
        P("tensor", None),
        P(),
        P(),
        P("dp", ("ctx", "tensor"), None),
        P(("ctx", "tensor"), None, "dp"),
        P(("ctx", "tensor"), None, "dp"),
        P(("ctx", "tensor"), "dp", None),
    )
    out_specs = P("dp", ("ctx", "tensor"), None)
    return jax.shard_map(
        on_device, mesh=mesh, in_specs=in_specs, out_specs=out_specs, check_vma=False
    )
```

```python
import functools

import jax
import jax.numpy as jnp
from jax import lax
from jax.experimental import pallas as pl
from jax.experimental.pallas import tpu as pltpu
from jax.sharding import PartitionSpec as P

QH = 32
KVH = 2
HEAD_WIDTH = 128
LANES = 128
DOWN_TILE = 512
UP_VMEM = 36 * 1024 * 1024
UP_SLOTS = 3
GROUP = 256
UP_PARTS = 4
SMALL_VMEM = 4 * 1024 * 1024
DOWN_VMEM = 20 * 1024 * 1024


def rotate(rows, places):
    length = rows.shape[0]
    values = rows.astype(jnp.float32).reshape(length, -1, HEAD_WIDTH)
    half = HEAD_WIDTH // 2
    freqs = jnp.power(
        jnp.float32(1000000.0), -(jnp.arange(half).astype(jnp.float32) * 2.0 / HEAD_WIDTH)
    )
    angles = places.astype(jnp.float32)[:, None] * freqs[None, :]
    cosine = jnp.cos(angles)[:, None, :]
    sine = jnp.sin(angles)[:, None, :]
    first = values[..., :half]
    second = values[..., half:]
    turned = jnp.concatenate(
        [first * cosine - second * sine, second * cosine + first * sine], axis=-1
    )
    return turned.astype(jnp.bfloat16)


def swap(block, axis, bits):
    pairs = [(i, i ^ bits) for i in range(lax.axis_size(axis))] if isinstance(bits, int) else bits
    return lax.ppermute(block, axis, pairs)


def add(*terms):
    total = terms[0].astype(jnp.float32)
    for term in terms[1:]:
        total = total + term.astype(jnp.float32)
    return total.astype(jnp.bfloat16)


def exchange(moves, flag):
    *blocks, flag = lax.optimization_barrier((*[move[0] for move in moves], flag))
    return [swap(block, axis, bits) for block, (_, axis, bits) in zip(blocks, moves)], flag


def fence_kernel(flag_ref, *refs):
    refs[-1][...] = flag_ref[...]


def fence(flag, earlier, resident=()):
    vmem = pl.BlockSpec(memory_space=pltpu.VMEM)
    hbm = pl.BlockSpec(memory_space=pl.ANY)
    return pl.pallas_call(
        fence_kernel,
        out_shape=jax.ShapeDtypeStruct(flag.shape, flag.dtype),
        in_specs=[vmem] + [hbm] * len(earlier) + [vmem] * len(resident),
        out_specs=vmem,
        compiler_params=pltpu.CompilerParams(vmem_limit_bytes=UP_VMEM if resident else SMALL_VMEM),
        cost_estimate=pl.CostEstimate(flops=20_000_000_000, bytes_accessed=0, transcendentals=0),
    )(flag, *earlier, *resident)


def halves_kernel(first_ref, second_ref, upper_ref, lower_ref):
    middle = upper_ref.shape[0]
    upper_ref[...] = first_ref[:middle]
    lower_ref[...] = second_ref[middle:]


def halves(first, second):
    rows, width = first.shape
    vmem = pl.BlockSpec(memory_space=pltpu.VMEM)
    shape = jax.ShapeDtypeStruct((rows // 2, width), first.dtype)
    return pl.pallas_call(
        halves_kernel,
        out_shape=[shape] * 2,
        in_specs=[vmem] * 2,
        out_specs=[vmem] * 2,
        compiler_params=pltpu.CompilerParams(vmem_limit_bytes=SMALL_VMEM),
    )(first, second)


def join_kernel(first_ref, second_ref, upper_ref, lower_ref, one_ref, other_ref):
    middle = upper_ref.shape[0]

    def plus(rows, more):
        return (rows.astype(jnp.float32) + more.astype(jnp.float32)).astype(jnp.bfloat16)

    one_ref[:middle] = plus(first_ref[:middle], upper_ref[...])
    one_ref[middle:] = first_ref[middle:]
    other_ref[:middle] = second_ref[:middle]
    other_ref[middle:] = plus(second_ref[middle:], lower_ref[...])


def join(first, second, upper, lower):
    vmem = pl.BlockSpec(memory_space=pltpu.VMEM)
    shape = jax.ShapeDtypeStruct(first.shape, first.dtype)
    return pl.pallas_call(
        join_kernel,
        out_shape=[shape] * 2,
        in_specs=[vmem] * 4,
        out_specs=[vmem] * 2,
        compiler_params=pltpu.CompilerParams(vmem_limit_bytes=SMALL_VMEM),
    )(first, second, upper, lower)


def fold(rows, size):
    bits = 2
    while bits < size:
        rows = [jnp.concatenate(rows, axis=0)]
        rows = [jnp.concatenate([rows[0], swap(rows[0], "tensor", bits)], axis=0)]
        bits *= 2
    return rows


def unfold(pieces, size):
    bits = size // 2
    while bits > 1:
        half = pieces[0].shape[0] // 2
        pieces = [add(pieces[0][:half], swap(pieces[0][half:], "tensor", bits))]
        bits //= 2
    if len(pieces) > 1:
        return pieces
    rows = pieces[0].shape[0]
    return jnp.split(pieces[0], [rows // 4, rows // 2, rows * 3 // 4, rows * 7 // 8])


def up_kernel(count, later, *refs):
    x_refs, refs = refs[:count], refs[count:]
    mine_ref, refs = refs[0], refs[1 + later :]
    gate_refs, up_refs, refs = refs[0:2], refs[2:4], refs[4:]
    *hidden_refs, rows_in, weights, rows_sem, weights_sem = refs
    experts, width, units = gate_refs[0].shape
    row_copies, start = [], 0
    for n, x_ref in enumerate(x_refs):
        rows = x_ref.shape[0]
        row_copies.append(pltpu.make_async_copy(x_ref, rows_in.at[pl.ds(start, rows), :], rows_sem.at[n]))
        start += rows

    def parts_of(e):
        return UP_PARTS if e == 0 else 1

    def weight_copies(e, part):
        size = width // parts_of(e)
        span = pl.ds(part * size, size)
        return [
            pltpu.make_async_copy(
                ref.at[e % experts, span, :],
                weights.at[e % UP_SLOTS, span, pl.ds(side * units, units)],
                weights_sem.at[e % UP_SLOTS, part, side],
            )
            for side, ref in enumerate((gate_refs[e // experts], up_refs[e // experts]))
        ]

    def start_weights(e):
        if e < 2 * experts:
            for part in range(parts_of(e)):
                for copy in weight_copies(e, part):
                    copy.start()

    for copy in row_copies:
        copy.start()
    for e in range(UP_SLOTS - 1):
        start_weights(e)
    for copy in row_copies:
        copy.wait()
    for e in range(2 * experts):
        start_weights(e + UP_SLOTS - 1)
        for group in range(0, rows_in.shape[0], GROUP):
            rows = slice(group, group + GROUP)
            both = None
            for part in range(parts_of(e)):
                if group == 0:
                    for copy in weight_copies(e, part):
                        copy.wait()
                size = width // parts_of(e)
                span = slice(part * size, (part + 1) * size)
                term = jnp.dot(
                    rows_in[rows, span], weights[e % UP_SLOTS, span], preferred_element_type=jnp.float32
                )
                both = term if both is None else both + term
            gate_val, up_val = both[:, :units], both[:, units:]
            spare = rows_in[rows, width:].astype(jnp.float32)
            weight = jnp.sum(spare * mine_ref[e : e + 1, :], axis=1, keepdims=True)
            value = gate_val / (1.0 + jnp.exp(-gate_val)) * up_val * weight
            hidden_refs[group // GROUP][:, e * units : (e + 1) * units] = value.astype(jnp.bfloat16)


def up_block(pieces, mine, later, gates, ups):
    experts, width, units = gates[0].shape
    rows = sum(piece.shape[0] for piece in pieces)
    vmem = pl.BlockSpec(memory_space=pltpu.VMEM)
    hbm = pl.BlockSpec(memory_space=pl.ANY)
    return pl.pallas_call(
        functools.partial(up_kernel, len(pieces), len(later)),
        out_shape=[jax.ShapeDtypeStruct((GROUP, 2 * experts * units), jnp.bfloat16)] * (rows // GROUP),
        in_specs=[hbm] * len(pieces) + [vmem] + [hbm] * (len(later) + 4),
        out_specs=[vmem] * (rows // GROUP),
        scratch_shapes=[
            pltpu.VMEM((rows, pieces[0].shape[1]), jnp.bfloat16),
            pltpu.VMEM((UP_SLOTS, width, 2 * units), jnp.bfloat16),
            pltpu.SemaphoreType.DMA((len(pieces),)),
            pltpu.SemaphoreType.DMA((UP_SLOTS, UP_PARTS, 2)),
        ],
        compiler_params=pltpu.CompilerParams(vmem_limit_bytes=UP_VMEM),
        cost_estimate=pl.CostEstimate(
            flops=8 * rows * experts * units * width,
            bytes_accessed=8 * experts * units * width + 2 * rows * width,
            transcendentals=2 * rows * experts * units,
        ),
    )(*pieces, mine, *later, *gates, *ups)


def down_kernel(count, later, hidden_ref, *refs):
    down_refs, refs = refs[later : later + 2], refs[later + 2 :]
    y_refs, (weights, weights_sem) = refs[:count], refs[count:]
    experts, units, width = down_refs[0].shape
    tiles = width // DOWN_TILE
    copies = [
        [
            pltpu.make_async_copy(
                down_refs[e // experts].at[e % experts, :, pl.ds(tile * DOWN_TILE, DOWN_TILE)],
                weights.at[tile, pl.ds(e * units, units), :],
                weights_sem.at[tile, e],
            )
            for e in range(2 * experts)
        ]
        for tile in range(tiles)
    ]
    for group in copies:
        for copy in group:
            copy.start()
    for tile in range(tiles):
        for copy in copies[tile]:
            copy.wait()
        cols = slice(tile * DOWN_TILE, (tile + 1) * DOWN_TILE)
        result = jnp.dot(
            hidden_ref[...], weights[tile], preferred_element_type=jnp.float32
        ).astype(jnp.bfloat16)
        start = 0
        for y_ref in y_refs:
            rows = y_ref.shape[0]
            y_ref[:, cols] = result[start : start + rows]
            start += rows


def down_block(hidden, sizes, later, downs):
    experts, units, width = downs[0].shape
    rows = hidden.shape[0]
    vmem = pl.BlockSpec(memory_space=pltpu.VMEM)
    hbm = pl.BlockSpec(memory_space=pl.ANY)
    return pl.pallas_call(
        functools.partial(down_kernel, len(sizes), len(later)),
        out_shape=[jax.ShapeDtypeStruct((size, width), jnp.bfloat16) for size in sizes],
        in_specs=[vmem] + [hbm] * (len(later) + 2),
        out_specs=[vmem] * len(sizes),
        scratch_shapes=[
            pltpu.VMEM((width // DOWN_TILE, 2 * experts * units, DOWN_TILE), jnp.bfloat16),
            pltpu.SemaphoreType.DMA((width // DOWN_TILE, 2 * experts)),
        ],
        compiler_params=pltpu.CompilerParams(vmem_limit_bytes=DOWN_VMEM),
        cost_estimate=pl.CostEstimate(
            flops=4 * rows * experts * units * width,
            bytes_accessed=4 * experts * units * width + 2 * rows * width,
            transcendentals=0,
        ),
    )(hidden, *later, *downs)


def on_device(
    query_rows,
    key_rows,
    value_rows,
    residual,
    out_proj,
    post_gain,
    router,
    routes,
    w_gate,
    w_up,
    w_down,
):
    gates_pair, ups_pair = [(w, swap(w, "tensor", 1)) for w in (w_gate, w_up)]
    local_tokens = query_rows.shape[1]
    local_heads = query_rows.shape[2] // HEAD_WIDTH
    group = QH // KVH
    kv_dev = max(1, local_heads // group)
    share = local_heads // kv_dev
    kv_first = lax.axis_index("tensor") * local_heads // group * HEAD_WIDTH
    my_ctx = lax.axis_index("ctx")
    pair = jnp.concatenate(
        [
            lax.dynamic_slice_in_dim(rows[0], kv_first, kv_dev * HEAD_WIDTH, axis=1)
            for rows in (key_rows, value_rows)
        ],
        axis=1,
    )
    contexts = lax.axis_size("ctx")
    pairs = jnp.concatenate([pair] + [swap(pair, "ctx", bits) for bits in range(1, contexts)], axis=0)
    within = jnp.arange(local_tokens)
    places = my_ctx * local_tokens + within
    key_places = jnp.concatenate([(my_ctx ^ bits) * local_tokens + within for bits in range(contexts)])
    qrot = rotate(query_rows[0], places).reshape(local_tokens, kv_dev, share, HEAD_WIDTH)
    krot = rotate(pairs[:, : kv_dev * HEAD_WIDTH], key_places)
    value_heads = pairs[:, kv_dev * HEAD_WIDTH :].reshape(-1, kv_dev, HEAD_WIDTH)
    attention_score = jnp.einsum(
        "qghd,kgd->ghqk", qrot, krot, preferred_element_type=jnp.float32
    ) / jnp.sqrt(jnp.float32(HEAD_WIDTH))
    causal = places[:, None] >= key_places[None, :]
    attention_score = jnp.where(causal, attention_score, jnp.float32(-1e30))
    peak = jnp.max(attention_score, axis=-1, keepdims=True)
    expon = jnp.where(causal, jnp.exp(attention_score - peak), jnp.float32(0.0))
    total = jnp.sum(expon, axis=-1)
    softmax_weights = expon.astype(jnp.bfloat16)
    summed_output = jnp.einsum(
        "ghqk,kgd->qghd", softmax_weights, value_heads, preferred_element_type=jnp.float32
    )
    attended = (
        (summed_output / jnp.transpose(total, (2, 0, 1))[..., None])
        .astype(jnp.bfloat16)
        .reshape(local_tokens, local_heads * HEAD_WIDTH)
    )
    projected = jnp.dot(attended, out_proj, preferred_element_type=jnp.float32)
    projected, other_gate, other_up = lax.optimization_barrier((projected, gates_pair[1], ups_pair[1]))
    gates_pair, ups_pair = (gates_pair[0], other_gate), (ups_pair[0], other_up)
    bits = lax.axis_size("tensor") // 2
    while bits:
        half = projected.shape[0] // 2
        high = (lax.axis_index("tensor") & bits) != 0
        keep = jnp.where(high, projected[half:], projected[:half])
        give = jnp.where(high, projected[:half], projected[half:])
        projected = keep + swap(give, "tensor", bits)
        bits //= 2
    mixed_wide = residual[0].astype(jnp.float32) + projected
    mixed = mixed_wide.astype(jnp.bfloat16)
    mixed, w_down = lax.optimization_barrier((mixed, w_down))
    downs_pair = w_down, swap(w_down, "tensor", 1)
    mixed_wide = mixed.astype(jnp.float32)
    scale = lax.rsqrt(jnp.mean(mixed_wide * mixed_wide, axis=-1, keepdims=True) + 1e-06)
    normed = (mixed_wide * scale * post_gain.astype(jnp.float32)).astype(jnp.bfloat16)
    logits = jnp.dot(normed, router, preferred_element_type=jnp.float32)
    picks = routes[0]
    tokens = picks.shape[0]
    experts_all = router.shape[1]
    chosen = jnp.any(picks[:, :, None] == jnp.arange(experts_all)[None, None, :], axis=1)
    peak_logit = jnp.max(jnp.where(chosen, logits, -jnp.inf), axis=1, keepdims=True)
    numer = jnp.where(chosen, jnp.exp(jnp.where(chosen, logits - peak_logit, 0.0)), 0.0)
    gates = numer / jnp.sum(numer, axis=1, keepdims=True)
    gates_high = gates.astype(jnp.bfloat16)
    gates_low = (gates - gates_high.astype(jnp.float32)).astype(jnp.bfloat16)
    lanes = -(-2 * experts_all // LANES) * LANES
    spare = jnp.zeros((tokens, lanes - 2 * experts_all), jnp.bfloat16)
    block = jnp.concatenate([normed, gates_high, gates_low, spare], axis=1)

    exp_dev = w_gate.shape[0]
    lane = jnp.arange(lanes)
    mine = []
    for core in (0, 1):
        group_id = lax.axis_index("ctx") * lax.axis_size("tensor") + (lax.axis_index("tensor") ^ core)
        for e in range(exp_dev):
            expert = group_id * exp_dev + e
            mine.append((lane == expert) | (lane == experts_all + expert))
    mine = jnp.stack(mine).astype(jnp.float32)

    cores = lax.axis_size("tensor")

    def out_near(rows):
        return [(rows, "ctx", 1), (rows, "ctx", 2)]

    def out_corner(near):
        upper, lower = halves(*near)
        return [(upper, "ctx", 2), (lower, "ctx", 1)]

    def back_corner(sums):
        return [(sums[3], "ctx", 2), (sums[4], "ctx", 1)]

    def back_near(sums, corner):
        first, second = join(sums[1], sums[2], *corner)
        return [(first, "ctx", 1), (second, "ctx", 2)]

    def up_of(blocks, later=()):
        pieces = [fold([own, *near, *corner], cores) for own, near, corner in blocks]
        sizes = [[piece.shape[0] for piece in group] for group in pieces]
        return up_block(sum(pieces, []), flag, later, gates_pair, ups_pair), sizes

    def down_of(hidden, n=0, later=()):
        rows, sizes = hidden
        return unfold(down_block(rows[n], sizes[n], later, downs_pair), cores)

    inward, outward = [(1, 2), (2, 1)], [(1, 0), (2, 3)]
    place = lax.axis_index("dp")
    inner = (place == 1) | (place == 2)

    flag = fence(mine, [block])
    (*near0, rows1, inner3), mine = exchange([*out_near(block), (block, "dp", 1), (block, "dp", inward)], mine)
    flag, other_down = lax.optimization_barrier((flag, downs_pair[1]))
    downs_pair = downs_pair[0], other_down
    (*got, inner2, outer2), flag = exchange(
        [*out_corner(near0), *out_near(rows1), (rows1, "dp", inward), (inner3, "dp", outward)], flag
    )
    corner0, near1 = got[:2], got[2:]
    rows2 = jnp.where(inner, inner2, outer2)
    flag = fence(flag, [*near0, rows1])
    (*got, outer3), flag = exchange([*out_corner(near1), *out_near(rows2), (inner2, "dp", outward)], flag)
    corner1, near2 = got[:2], got[2:]
    rows3 = jnp.where(inner, inner3, outer3)
    hidden0 = up_of([(block, near0, corner0)])
    got, _ = exchange([*out_corner(near2), *out_near(rows3)], hidden0[0][0])
    corner2, near3 = got[:2], got[2:]
    hidden1 = up_of([(rows1, near1, corner1)], [hidden0[0][0], *near2, rows3])
    sums1 = down_of(hidden1, 0, near3)
    half1, _ = exchange(back_corner(sums1), flag)
    out3 = out_corner(near3)
    corner3, _ = exchange(out3, flag)
    hidden2 = up_of([(rows2, near2, corner2)], [sums1[0], out3[0][0]])
    *half1, _ = lax.optimization_barrier((*half1, hidden2[0][0]))
    back1 = back_near(sums1, half1)
    full1, _ = exchange(back1, flag)
    sums2 = down_of(hidden2, 0, [back1[0][0], corner3[0]])
    half2, _ = exchange(back_corner(sums2), flag)
    sums0 = down_of(hidden0, 0, [sums2[0]])
    back2 = back_near(sums2, half2)
    full2, _ = exchange(back2, flag)
    hidden3 = up_of([(rows3, near3, corner3)], [back2[0][0], *full1, sums0[0]])
    part1 = swap(add(sums1[0], *full1), "dp", 1)
    total2 = add(sums2[0], *full2)
    sums3 = down_of(hidden3, 0, [total2, part1])
    half0, _ = exchange(back_corner(sums0), hidden3[0][0])
    (upper3, *_), (lower3, *_) = back_corner(sums3)
    upper3, lower3, *half0 = lax.optimization_barrier((upper3, lower3, *half0))
    half3 = [swap(upper3, "ctx", 2), swap(lower3, "ctx", 1)]
    part2 = swap(total2, "dp", 2)
    back3 = back_near(sums3, half3)
    full3, _ = exchange(back3, flag)
    *full3, part2 = lax.optimization_barrier((*full3, part2))
    total3 = add(sums3[0], *full3)
    (part3,), part2 = exchange([(total3, "dp", 3)], part2)
    *half0, _ = lax.optimization_barrier((*half0, total3))
    full0, _ = exchange(back_near(sums0, half0), total3)
    moe_sum = sums0[0].astype(jnp.float32)
    for part in (*full0, part1, part2, part3):
        moe_sum = moe_sum + part.astype(jnp.float32)
    layer_out = (mixed_wide + moe_sum).astype(jnp.bfloat16)
    return layer_out[None]


def solution(mesh):
    in_specs = (
        P("dp", "ctx", "tensor"),
        P("dp", "ctx", None),
        P("dp", "ctx", None),
        P("dp", ("ctx", "tensor"), None),
        P("tensor", None),
        P(),
        P(),
        P("dp", ("ctx", "tensor"), None),
        P(("ctx", "tensor"), None, "dp"),
        P(("ctx", "tensor"), None, "dp"),
        P(("ctx", "tensor"), "dp", None),
    )
    out_specs = P("dp", ("ctx", "tensor"), None)
    return jax.shard_map(
        on_device, mesh=mesh, in_specs=in_specs, out_specs=out_specs, check_vma=False
    )
```
